256 devices in a mesh: expert: 64 (over x, z, core), dp: 4 (over y).
Axes of the slice: x: 4, y: 4, z: 8, core: 2. Of those that a mesh axis runs over, the one named last changes fastest.
Arguments:
- tokens: bfloat16 [2048, 7168], P(('expert', 'dp')), may hold values from -6 to 6
- out_grads: bfloat16 [2048, 7168], P(('expert', 'dp')), may hold values from -4 to 4
- expert_ids: int32 [2048, 8], P('expert'), may hold values from 0 to 63, all different within a row; in each aligned block of 8 rows (0 to 7, 8 to 15, ...) at most 2 rows name the same one
- gates: bfloat16 [2048, 8], P('expert'), may hold values from 0.019897461 to 0.29882812
- w_gate: bfloat16 [64, 7168, 1024], P('expert', None, 'dp'), may hold values from -0.0625 to 0.0625
- w_up: bfloat16 [64, 7168, 1024], P('expert', None, 'dp'), may hold values from -0.0625 to 0.0625
- w_down: bfloat16 [64, 1024, 7168], P('expert', 'dp'), may hold values from -0.1875 to 0.1875
Outputs:
- input_grads: bfloat16 [2048, 7168], P(('expert', 'dp'))
- fisher: float32 [64], P('expert')
The draws below stay inside these ranges and needn't reach their ends.
Inputs may be any that keep to these rules, and one draw needn't show every extreme that they name: `expert_ids`: each row names 8 different experts. In each aligned block of 8 rows no expert is named by more than 2 rows, a bound that some block reaches.
All inputs are finite; a program needn't handle non-finite values.
Results may differ from the reference program's by a relative error of at most 0.015.
Values may be sent and summed in bfloat16 or wider, within the bound.
A program may use at most 128 MiB of HBM per device.

```python
import math
import jax
import jax.numpy as jnp
import numpy as np
from jax import lax

D = 7168
FF = 1024
TOP = 8
TOK_DEV = 8
EXPERTS = 64
TOKENS = 2048
CAP = 2
N_DP = 4


def steps_of(rng, dims, split, smallest, largest):
    def one(dim, parts):
        heights = jax.random.uniform(jax.random.fold_in(jax.random.fold_in(rng, 6), dim), (parts,), jnp.float32, smallest / len(split), largest / len(split))
        return jnp.repeat(jnp.exp(heights), dims[dim] // parts).reshape((-1,) + (1,) * (len(dims) - dim - 1))

    loudness = one(*split[0])
    for cut in split[1:]:
        loudness = loudness * one(*cut)
    return loudness


def routed_block(key, own, number, rows, count, top, bound, slope):
    order = jax.random.permutation(key, count)
    packed, usual = portions_of(count, rows * top, bound, slope, True), portions_of(count, rows * top, bound, slope, False)
    places = jnp.arange(count)

    def named(sizes, turn):
        used = int((sizes > 0).sum())
        fixed = max(1, used // 4)
        shifted = fixed + (places - fixed + turn * (used - fixed)) % max(1, count - fixed)
        return jnp.zeros((count,), jnp.int32).at[order[jnp.where(places < fixed, places, shifted)]].set(jnp.asarray(sizes, jnp.int32))

    sizes = jnp.where(number % 4 == 0, named(packed, number // 4), named(usual, number - number // 4 - 1))
    mixed = jax.random.permutation(jax.random.fold_in(own, 3), count)
    giver, taker = mixed[0:count // 2 * 2:2], mixed[1:count // 2 * 2:2]
    slack = jnp.minimum(sizes[giver] - 1, bound - sizes[taker]) // 2
    slack = jnp.where((giver == order[0]) | (taker == order[0]) | (sizes[taker] == 0), 0, jnp.maximum(slack, 0))
    shifted = jax.random.randint(jax.random.fold_in(own, 4), (count // 2,), 0, 1 << 20) % (slack + 1)
    sizes = sizes.at[giver].add(-shifted).at[taker].add(shifted)
    labels = jnp.searchsorted(jnp.cumsum(sizes), jnp.arange(rows * top), side="right").astype(jnp.int32)
    table = labels.reshape(top, rows).T
    table = table[jax.random.permutation(jax.random.fold_in(own, 1), rows)]
    turn = jax.random.randint(jax.random.fold_in(own, 2), (rows, 1), 0, top)
    return jnp.take_along_axis(table, (jnp.arange(top)[None, :] + turn) % top, axis=1)


def portions_of(amount, total, limit, lean, full):
    portions = [(1 << 20) // math.isqrt(grade ** lean) + 1 for grade in range(1, amount + 1)]
    largest = limit if full else min(limit, max(-(-total // amount), total * portions[0] // sum(portions)))
    least = 1 if total - largest >= amount - 1 else 0
    counts, rest = [largest] + [least] * (amount - 1), total - largest - least * (amount - 1)
    while rest > 0:
        free = [i for i in range(1, amount) if counts[i] < largest] or [i for i in range(1, amount) if counts[i] < limit]
        pool, left = sum([portions[i] for i in free]), rest
        for i in free:
            extra = min(limit - counts[i], max(1, left * portions[i] // pool), rest)
            counts[i] = counts[i] + extra
            rest = rest - extra
    return np.array(counts)


def bell_draw(rng, dims, deviation, reach, pieces=(), kind=jnp.bfloat16):
    values = jax.random.normal(rng, dims, jnp.float32) * deviation
    if len(pieces) > 0:
        values = steps_of(rng, dims, pieces, -0.22, 0.18) * values
    return jnp.clip(values, min=-reach, max=reach).astype(kind)


def setup_inputs(seed: int = 0) -> dict:
    keys = jax.random.split(jax.random.key(seed), 8)
    tokens = bell_draw(keys[0], (TOKENS, D), 1.0, 6.0, ((0, 256),))
    out_grads = bell_draw(keys[1], (TOKENS, D), 0.5, 4.0, ((0, 256),))
    expert_ids_keys = jax.random.split(jax.random.fold_in(keys[2], 1), TOKENS // TOK_DEV)
    expert_ids_turns = jax.random.permutation(jax.random.fold_in(keys[2], 3), TOKENS // TOK_DEV)
    expert_ids = jax.vmap(lambda own, number: routed_block(jax.random.fold_in(keys[2], 2), own, number, TOK_DEV, EXPERTS, TOP, CAP, 2))(expert_ids_keys, expert_ids_turns).reshape((TOKENS, TOP))
    gates = jnp.clip(jnp.exp(math.log(0.29882812) - 2.7092764 * jax.random.uniform(keys[3], (TOKENS, TOP), jnp.float32) ** steps_of(keys[3], (TOKENS, TOP), ((0, 64),), -0.2, 0.2)), 0.019897461, 0.29882812).astype(jnp.bfloat16)
    w_gate = bell_draw(keys[4], (EXPERTS, D, FF), D ** -0.5, 0.0625, ((0, 64), (2, 4)))
    w_up = bell_draw(keys[5], (EXPERTS, D, FF), D ** -0.5, 0.0625, ((0, 64), (2, 4)))
    w_down = bell_draw(keys[6], (EXPERTS, FF, D), FF ** -0.5, 0.1875, ((0, 64), (1, 4)))
    return dict(tokens=tokens, out_grads=out_grads, expert_ids=expert_ids, gates=gates, w_gate=w_gate, w_up=w_up, w_down=w_down)


def reference(tokens, out_grads, expert_ids, gates, w_gate, w_up, w_down):
    slot_total = (TOKENS // TOK_DEV) * CAP
    block_width = FF // N_DP
    scale_factor = EXPERTS / (TOKENS * TOP)

    def per_expert(totals, expert):
        hits = expert_ids == expert
        weight_all = jnp.sum(jnp.where(hits, gates.astype(jnp.float32), jnp.float32(0.0)), axis=1)
        chosen = jnp.nonzero(jnp.any(hits, axis=1), size=slot_total, fill_value=TOKENS)[0].astype(jnp.int32)
        valid = chosen < TOKENS
        safe_rows = jnp.minimum(chosen, TOKENS - 1).astype(jnp.int32)
        weights = jnp.where(valid, weight_all[safe_rows], jnp.float32(0.0))
        token_rows = tokens[safe_rows].astype(jnp.float32)
        grad_rows = out_grads[safe_rows].astype(jnp.float32)
        gate_mat = w_gate[expert].astype(jnp.float32)
        up_mat = w_up[expert].astype(jnp.float32)
        down_mat = w_down[expert].astype(jnp.float32)
        gate_pre = jnp.dot(token_rows, gate_mat)
        up_pre = jnp.dot(token_rows, up_mat)
        down_back = jnp.dot(grad_rows, down_mat.T)
        sigmoid_a = jax.nn.sigmoid(gate_pre)
        active = gate_pre * sigmoid_a
        dots = jnp.sum(active * up_pre * down_back, axis=1)
        d_gate = (down_back * up_pre * sigmoid_a * (1.0 + gate_pre * (1.0 - sigmoid_a))).astype(jnp.bfloat16)
        d_up = (down_back * active).astype(jnp.bfloat16)
        part = jnp.einsum("mpj,dpj->pmd", d_gate.astype(jnp.float32).reshape(slot_total, N_DP, block_width),
                          gate_mat.reshape(D, N_DP, block_width))
        part = part + jnp.einsum("mpj,dpj->pmd", d_up.astype(jnp.float32).reshape(slot_total, N_DP, block_width),
                                 up_mat.reshape(D, N_DP, block_width))
        rounded = lax.optimization_barrier(part.astype(jnp.bfloat16))
        back = jnp.sum(rounded.astype(jnp.float32), axis=0).astype(jnp.bfloat16)
        fisher_value = jnp.sum(jnp.where(valid, (weights * dots) ** 2, jnp.float32(0.0))) * scale_factor
        totals = totals.at[chosen].add(weights[:, None] * back.astype(jnp.float32), mode="drop")
        return totals, fisher_value

    totals, fisher = lax.scan(per_expert, jnp.zeros((TOKENS, D), jnp.float32),
                              jnp.arange(EXPERTS, dtype=jnp.int32))
    return totals.astype(jnp.bfloat16), fisher
```

```python
import functools

import jax
import jax.numpy as jnp
from jax import lax
from jax.experimental import pallas as pl
from jax.experimental.pallas import tpu as pltpu
from jax.sharding import PartitionSpec as P

F32, BF16 = jnp.float32, jnp.bfloat16
NX, NZ, NC, NY = 4, 8, 2, 4
META = 128
MESH = pl.DeviceIdType.MESH


def position():
    e = lax.axis_index("expert")
    return lax.div(e, NZ * NC), lax.rem(lax.div(e, NC), NZ), lax.rem(e, NC), lax.axis_index("dp")


def place(x, z, c, y):
    return {"expert": (x * NZ + z) * NC + c, "dp": y}


def remote(src, dst, send, recv, device):
    return pltpu.make_async_remote_copy(
        src_ref=src, dst_ref=dst, send_sem=send, recv_sem=recv, device_id=device, device_id_type=MESH
    )


def meet(peers):
    barrier = pltpu.get_barrier_semaphore()
    for peer in peers:
        pl.semaphore_signal(barrier, inc=1, device_id=peer, device_id_type=MESH)
    pl.semaphore_wait(barrier, len(peers))


def dot_nt(left, right):
    return lax.dot_general(left, right, (((1,), (1,)), ((), ())), preferred_element_type=F32)


def forward_kernel(
    chunks, blk, wg_hbm, wu_hbm, wd_hbm, da_ref, db_ref, sg_ref, un_ref,
    G, R, S, wg, wu, wd, acc, lsem, zs, zr, xs, xr, cs, cr, ys, yr,
):
    x, z, c, y = position()
    e = lax.axis_index("expert")
    nc = len(chunks)
    xp, xm, xa = lax.rem(x + 1, NX), lax.rem(x + NX - 1, NX), lax.rem(x + 2, NX)
    zp, zm = lax.rem(z + 1, NZ), lax.rem(z + NZ - 1, NZ)
    yp, ym, ya = lax.rem(y + 1, NY), lax.rem(y + NY - 1, NY), lax.rem(y + 2, NY)
    co = 1 - c
    dxp, dxm = place(xp, z, c, y), place(xm, z, c, y)
    dzp, dzm = place(x, zp, c, y), place(x, zm, c, y)
    dyp, dym = place(x, z, c, yp), place(x, z, c, ym)
    dco = place(x, z, co, y)
    loads = [
        pltpu.make_async_copy(wg_hbm, wg, lsem.at[0]),
        pltpu.make_async_copy(wu_hbm, wu, lsem.at[1]),
        pltpu.make_async_copy(wd_hbm, wd, lsem.at[2]),
    ]
    for load in loads:
        load.start()
    G[x, c, z] = blk[...]
    meet([dxp, dxm, dzp, dzm, dyp, dym, dco])
    sent = []

    def go(copy):
        copy.start()
        sent.append(copy)

    def cols(h):
        return pl.ds(chunks[h][0], chunks[h][1])

    def halves(h):
        start, size = chunks[h]
        first = size // 2 // 128 * 128
        return pl.ds(start, first), pl.ds(start + first, size - first)

    def zblock(h, off):
        return G.at[x, c, lax.rem(z + off + NZ, NZ), :, cols(h)]

    def z_send(h, step):
        if step < 4:
            b = zblock(h, -step)
            go(remote(b, b, zs.at[h, step], zr.at[h, step], dzp))
        if step < 3:
            b = zblock(h, step)
            go(remote(b, b, zs.at[h, 4 + step], zr.at[h, 4 + step], dzm))

    def z_recv(h, step):
        if step < 4:
            b = zblock(h, -step - 1)
            remote(b, b, zs.at[h, step], zr.at[h, step], dzp).wait_recv()
        if step < 3:
            b = zblock(h, step + 1)
            remote(b, b, zs.at[h, 4 + step], zr.at[h, 4 + step], dzm).wait_recv()

    def z_advance(h, step):
        z_recv(h, step)
        if step < 3:
            z_send(h, step + 1)

    def line(h, xx, cc):
        return G.at[xx, cc, :, :, cols(h)]

    def part(xx, ds):
        return G.at[xx, c, :, :, ds]

    def share(h, k, xx):
        b = line(h, xx, c)
        go(remote(b, b, cs.at[h, k], cr.at[h, k], dco))

    def shared(h, k, xx):
        b = line(h, xx, co)
        remote(b, b, cs.at[h, k], cr.at[h, k], dco).wait_recv()

    def x_start(h):
        b = line(h, x, c)
        go(remote(b, b, xs.at[h, 0], xr.at[h, 0], dxp))
        go(remote(b, b, xs.at[h, 1], xr.at[h, 1], dxm))
        share(h, 0, x)

    def x_forward(h):
        lo, hi = halves(h)
        b = line(h, xm, c)
        remote(b, b, xs.at[h, 0], xr.at[h, 0], dxp).wait_recv()
        go(remote(part(xm, lo), part(xm, lo), xs.at[h, 2], xr.at[h, 2], dxp))
        share(h, 1, xm)
        b = line(h, xp, c)
        remote(b, b, xs.at[h, 1], xr.at[h, 1], dxm).wait_recv()
        go(remote(part(xp, hi), part(xp, hi), xs.at[h, 3], xr.at[h, 3], dxm))
        share(h, 2, xp)

    def x_last(h):
        lo, hi = halves(h)
        remote(part(xa, lo), part(xa, lo), xs.at[h, 2], xr.at[h, 2], dxp).wait_recv()
        remote(part(xa, hi), part(xa, hi), xs.at[h, 3], xr.at[h, 3], dxm).wait_recv()
        share(h, 3, xa)

    rows = NC * NZ * 16

    def routes(xx):
        meta = G[xx, :, :, :, 0:META].reshape(rows, META).astype(F32)
        lane = lax.broadcasted_iota(jnp.int32, (rows, META), 1)
        chosen = jnp.where(lane < 8, meta, -1.0) == e.astype(F32)
        gates = pltpu.roll(meta, META - 8, 1)
        hit = jnp.sum(chosen.astype(F32), axis=1, keepdims=True)
        gate = jnp.sum(jnp.where(chosen, gates, 0.0), axis=1, keepdims=True)
        r = lax.broadcasted_iota(jnp.int32, (rows, rows), 0)
        q = lax.broadcasted_iota(jnp.int32, (rows, rows), 1)
        earlier = jnp.where((r // 8 == q // 8) & (q < r), 1.0, 0.0).astype(BF16)
        hits = jnp.broadcast_to(hit, (rows, META))
        rank = jnp.dot(earlier, hits.astype(BF16), preferred_element_type=F32)
        r = lax.broadcasted_iota(jnp.int32, (rows, META), 0)
        base = (r // 8 % 2) * 32 + (r // 128) * 16 + (r // 16 % 8) * 2
        match = (lane.astype(F32) == base.astype(F32) + rank) & (hits > 0.5)
        pick = jnp.where(match, 1.0, 0.0)
        S[xx] = jnp.transpose(pick)[:64].astype(BF16)
        give = jnp.where(match, jnp.broadcast_to(gate, (rows, META)), 0.0)
        un_ref[xx] = give.reshape(16, 16, META)[:, :8].reshape(128, META).astype(BF16)

    def pack(h, xx):
        if h == 0:
            routes(xx)
        slab = G[xx, :, :, :, cols(h)].reshape(rows, chunks[h][1])
        got = jnp.dot(S[xx], slab, preferred_element_type=F32).astype(BF16)
        R[y, xx, :, :, cols(h)] = got.reshape(2, 32, chunks[h][1])

    def packed(g, xx, ds):
        return R.at[g, xx, :, :, ds]

    def y_send(h, k, xx):
        b = packed(y, xx, cols(h))
        go(remote(b, b, ys.at[h, k, 0], yr.at[h, k, 0], dyp))
        go(remote(b, b, ys.at[h, k, 1], yr.at[h, k, 1], dym))

    def y_forward(h, k, xx):
        lo, hi = halves(h)
        b = packed(ym, xx, cols(h))
        remote(b, b, ys.at[h, k, 0], yr.at[h, k, 0], dyp).wait_recv()
        b = packed(ym, xx, lo)
        go(remote(b, b, ys.at[h, k, 2], yr.at[h, k, 2], dyp))
        b = packed(yp, xx, cols(h))
        remote(b, b, ys.at[h, k, 1], yr.at[h, k, 1], dym).wait_recv()
        b = packed(yp, xx, hi)
        go(remote(b, b, ys.at[h, k, 3], yr.at[h, k, 3], dym))

    def y_last(h, k, xx):
        lo, hi = halves(h)
        b = packed(ya, xx, lo)
        remote(b, b, ys.at[h, k, 2], yr.at[h, k, 2], dyp).wait_recv()
        b = packed(ya, xx, hi)
        remote(b, b, ys.at[h, k, 3], yr.at[h, k, 3], dym).wait_recv()

    order = [x, xm, xp, xa]

    def multiply(h):
        start, size = chunks[h]
        if h == 0:
            start, size = META, size - META
            for load in loads:
                load.wait()
        f = pl.ds(start - META, size)
        at = pl.ds(start, size)
        tok = R[:, :, 0, :, at].reshape(512, size)
        grad = R[:, :, 1, :, at].reshape(512, size)
        a = jnp.dot(tok, wg[f, :], preferred_element_type=F32)
        b = jnp.dot(tok, wu[f, :], preferred_element_type=F32)
        u = dot_nt(grad, wd[:, f])
        if h == 0:
            acc[0], acc[1], acc[2] = a, b, u
        else:
            acc[0] += a
            acc[1] += b
            acc[2] += u

    z_send(0, 0)
    for step in range(4):
        z_advance(0, step)
    x_start(0)
    waiting = []
    for h in range(nc):
        more = h + 1 < nc
        if more:
            z_send(h + 1, 0)
        shared(h, 0, x)
        pack(h, x)
        y_send(h, 0, x)
        if waiting:
            y_forward(*waiting.pop(0))
        if more:
            z_advance(h + 1, 0)
        x_forward(h)
        if more:
            z_advance(h + 1, 1)
        shared(h, 1, xm)
        pack(h, xm)
        y_send(h, 1, xm)
        y_forward(h, 0, x)
        if more:
            z_advance(h + 1, 2)
        shared(h, 2, xp)
        pack(h, xp)
        y_send(h, 2, xp)
        if more:
            z_advance(h + 1, 3)
            x_start(h + 1)
        x_last(h)
        y_forward(h, 1, xm)
        shared(h, 3, xa)
        pack(h, xa)
        y_send(h, 3, xa)
        y_forward(h, 2, xp)
        waiting.append((h, 3, xa))
        if h:
            for k, xx in enumerate(order):
                y_last(h - 1, k, xx)
            multiply(h - 1)
    y_forward(*waiting.pop(0))
    for k, xx in enumerate(order):
        y_last(nc - 1, k, xx)
    multiply(nc - 1)
    lane = lax.broadcasted_iota(jnp.int32, (128, META), 1)
    for g in range(4):
        at = pl.ds(g * 128, 128)
        a, b, u = acc[0, at, :], acc[1, at, :], acc[2, at, :]
        sig = jax.nn.sigmoid(a)
        active = a * sig
        s = jnp.sum(active * b * u, axis=1, keepdims=True)
        da_ref[at, :] = (u * b * sig * (1.0 + a * (1.0 - sig))).astype(BF16)
        db_ref[at, :] = (u * active).astype(BF16)
        meta = R[g, :, 0, :, 0:META].reshape(128, META).astype(F32)
        chosen = jnp.where(lane < 8, meta, -1.0) == e.astype(F32)
        gate = jnp.sum(jnp.where(chosen, pltpu.roll(meta, META - 8, 1), 0.0), axis=1, keepdims=True)
        sg_ref[at, :] = jnp.where(lane == 0, s, jnp.where(lane == 1, gate, 0.0))
    for copy in sent:
        copy.wait_send()


def forward(blk, wg, wu, wd, pieces):
    width = blk.shape[1] - META
    step = width // pieces
    chunks = [(META + i * step, step) for i in range(pieces)]
    chunks[0] = (0, META + step)
    vm = pl.BlockSpec(memory_space=pltpu.VMEM)
    hbm = pl.BlockSpec(memory_space=pl.ANY)
    D = pltpu.SemaphoreType.DMA
    shape = jax.ShapeDtypeStruct
    return pl.pallas_call(
        functools.partial(forward_kernel, chunks),
        out_shape=(
            shape((512, 256), BF16), shape((512, 256), BF16), shape((512, META), F32),
            shape((NX, 128, META), BF16),
        ),
        in_specs=[vm, hbm, hbm, hbm],
        out_specs=(vm, vm, vm, vm),
        scratch_shapes=[
            pltpu.VMEM((NX, NC, NZ, 16, width + META), BF16),
            pltpu.VMEM((NY, NX, 2, 32, width + META), BF16),
            pltpu.VMEM((NX, 64, 256), BF16),
            pltpu.VMEM((width, 256), BF16), pltpu.VMEM((width, 256), BF16), pltpu.VMEM((256, width), BF16),
            pltpu.VMEM((3, 512, 256), F32),
            D((3,)), D((pieces, 7)), D((pieces, 7)), D((pieces, 4)), D((pieces, 4)),
            D((pieces, 4)), D((pieces, 4)), D((pieces, 4, 4)), D((pieces, 4, 4)),
        ],
        compiler_params=pltpu.CompilerParams(
            collective_id=1, has_side_effects=True, vmem_limit_bytes=60 << 20
        ),
        name="forward",
    )(blk, wg, wu, wd)


def times_transposed(left, right):
    return lax.dot_general(left, right, (((1,), (1,)), ((), ())), preferred_element_type=F32)


def per_device(tokens, out_grads, expert_ids, gates, w_gate, w_up, w_down):
    group = lax.axis_index("dp")
    ids = lax.dynamic_slice_in_dim(expert_ids, group * 8, 8, 0).astype(BF16)
    own_gates = lax.dynamic_slice_in_dim(gates, group * 8, 8, 0)
    meta = jnp.pad(jnp.concatenate([ids, own_gates], axis=1), ((0, 0), (0, META - 16)))
    blk = jnp.concatenate(
        [jnp.concatenate([meta, meta], axis=0), jnp.concatenate([tokens, out_grads], axis=0)], axis=1
    )
    gate_mat, up_mat, down_mat = w_gate[0], w_up[0], w_down[0]
    d_gate, d_up, sg, give = forward(blk, gate_mat, up_mat, down_mat, 4)
    dots = lax.psum(sg[:, 0], "dp")
    fisher = (jnp.sum((sg[:, 1] * dots) ** 2) * (1.0 / 256.0)).reshape(1)
    summed = (times_transposed(d_gate, gate_mat) + times_transposed(d_up, up_mat)).astype(BF16)
    back = lax.psum_scatter(summed, "dp", scatter_dimension=0, tiled=True)
    back = back.reshape(NX, NC, NZ, 2, -1).transpose(0, 2, 1, 3, 4).reshape(64, 2, -1)
    rows = lax.all_to_all(back, "expert", split_axis=0, concat_axis=0, tiled=True)
    gv = give[:, :, :32].reshape(NX, NC, NZ, 8, NC, NZ, 2)
    gv = jnp.einsum("xczrczk->xzcrk", gv.astype(F32)).astype(BF16)
    gv = lax.all_to_all(gv.reshape(64, 8, 2), "expert", split_axis=0, concat_axis=0, tiled=True)
    out = jnp.einsum("erk,ekd->rd", gv, rows, preferred_element_type=F32)
    return (out.astype(BF16), fisher)


def solution(mesh):
    placed = (
        P(("expert", "dp"), None), P(("expert", "dp"), None), P("expert", None), P("expert", None),
        P("expert", None, "dp"), P("expert", None, "dp"), P("expert", "dp", None),
    )
    return jax.shard_map(
        per_device, mesh=mesh, in_specs=placed,
        out_specs=(P(("expert", "dp"), None), P("expert")), check_vma=False,
    )
```

```python
import functools

import jax
import jax.numpy as jnp
from jax import lax
from jax.experimental import pallas as pl
from jax.experimental.pallas import tpu as pltpu
from jax.sharding import PartitionSpec as P

F32, BF16 = jnp.float32, jnp.bfloat16
NX, NZ, NC, NY = 4, 8, 2, 4
META = 128
FORWARD_PIECES, BACKWARD_PIECES = 4, 7
MESH = pl.DeviceIdType.MESH


def position():
    e = lax.axis_index("expert")
    return lax.div(e, NZ * NC), lax.rem(lax.div(e, NC), NZ), lax.rem(e, NC), lax.axis_index("dp")


def place(x, z, c, y):
    return {"expert": (x * NZ + z) * NC + c, "dp": y}


def remote(src, dst, send, recv, device):
    return pltpu.make_async_remote_copy(
        src_ref=src, dst_ref=dst, send_sem=send, recv_sem=recv, device_id=device, device_id_type=MESH
    )


def meet(peers):
    barrier = pltpu.get_barrier_semaphore()
    for peer in peers:
        pl.semaphore_signal(barrier, inc=1, device_id=peer, device_id_type=MESH)
    pl.semaphore_wait(barrier, len(peers))


def dot_nt(left, right):
    return lax.dot_general(left, right, (((1,), (1,)), ((), ())), preferred_element_type=F32)


def forward_kernel(
    chunks, blk, wg_hbm, wu_hbm, wd_hbm, da_ref, db_ref, sg_ref, un_ref,
    G, R, S, wg, wu, wd, acc, lsem, zs, zr, xs, xr, cs, cr, ys, yr,
):
    x, z, c, y = position()
    e = lax.axis_index("expert")
    nc = len(chunks)
    xp, xm, xa = lax.rem(x + 1, NX), lax.rem(x + NX - 1, NX), lax.rem(x + 2, NX)
    zp, zm = lax.rem(z + 1, NZ), lax.rem(z + NZ - 1, NZ)
    yp, ym, ya = lax.rem(y + 1, NY), lax.rem(y + NY - 1, NY), lax.rem(y + 2, NY)
    co = 1 - c
    dxp, dxm = place(xp, z, c, y), place(xm, z, c, y)
    dzp, dzm = place(x, zp, c, y), place(x, zm, c, y)
    dyp, dym = place(x, z, c, yp), place(x, z, c, ym)
    dco = place(x, z, co, y)
    loads = [
        pltpu.make_async_copy(wg_hbm, wg, lsem.at[0]),
        pltpu.make_async_copy(wu_hbm, wu, lsem.at[1]),
        pltpu.make_async_copy(wd_hbm, wd, lsem.at[2]),
    ]
    for load in loads:
        load.start()
    G[x, c, z] = blk[...]
    meet([dxp, dxm, dzp, dzm, dyp, dym, dco])
    sent = []

    def go(copy):
        copy.start()
        sent.append(copy)

    def cols(h):
        return pl.ds(chunks[h][0], chunks[h][1])

    def halves(h):
        start, size = chunks[h]
        first = size // 2 // 128 * 128
        return pl.ds(start, first), pl.ds(start + first, size - first)

    def zblock(h, off):
        return G.at[x, c, lax.rem(z + off + NZ, NZ), :, cols(h)]

    def z_send(h, step):
        if step < 4:
            b = zblock(h, -step)
            go(remote(b, b, zs.at[h, step], zr.at[h, step], dzp))
        if step < 3:
            b = zblock(h, step)
            go(remote(b, b, zs.at[h, 4 + step], zr.at[h, 4 + step], dzm))

    def z_recv(h, step):
        if step < 4:
            b = zblock(h, -step - 1)
            remote(b, b, zs.at[h, step], zr.at[h, step], dzp).wait_recv()
        if step < 3:
            b = zblock(h, step + 1)
            remote(b, b, zs.at[h, 4 + step], zr.at[h, 4 + step], dzm).wait_recv()

    def z_advance(h, step):
        z_recv(h, step)
        if step < 3:
            z_send(h, step + 1)

    def line(h, xx, cc):
        return G.at[xx, cc, :, :, cols(h)]

    def part(xx, ds):
        return G.at[xx, c, :, :, ds]

    def share(h, k, xx):
        b = line(h, xx, c)
        go(remote(b, b, cs.at[h, k], cr.at[h, k], dco))

    def shared(h, k, xx):
        b = line(h, xx, co)
        remote(b, b, cs.at[h, k], cr.at[h, k], dco).wait_recv()

    def x_start(h):
        b = line(h, x, c)
        go(remote(b, b, xs.at[h, 0], xr.at[h, 0], dxp))
        go(remote(b, b, xs.at[h, 1], xr.at[h, 1], dxm))
        share(h, 0, x)

    def x_forward(h):
        lo, hi = halves(h)
        b = line(h, xm, c)
        remote(b, b, xs.at[h, 0], xr.at[h, 0], dxp).wait_recv()
        go(remote(part(xm, lo), part(xm, lo), xs.at[h, 2], xr.at[h, 2], dxp))
        share(h, 1, xm)
        b = line(h, xp, c)
        remote(b, b, xs.at[h, 1], xr.at[h, 1], dxm).wait_recv()
        go(remote(part(xp, hi), part(xp, hi), xs.at[h, 3], xr.at[h, 3], dxm))
        share(h, 2, xp)

    def x_last(h):
        lo, hi = halves(h)
        remote(part(xa, lo), part(xa, lo), xs.at[h, 2], xr.at[h, 2], dxp).wait_recv()
        remote(part(xa, hi), part(xa, hi), xs.at[h, 3], xr.at[h, 3], dxm).wait_recv()
        share(h, 3, xa)

    rows = NC * NZ * 16

    def routes(xx):
        meta = G[xx, :, :, :, 0:META].reshape(rows, META).astype(F32)
        lane = lax.broadcasted_iota(jnp.int32, (rows, META), 1)
        chosen = jnp.where(lane < 8, meta, -1.0) == e.astype(F32)
        gates = pltpu.roll(meta, META - 8, 1)
        hit = jnp.sum(chosen.astype(F32), axis=1, keepdims=True)
        gate = jnp.sum(jnp.where(chosen, gates, 0.0), axis=1, keepdims=True)
        r = lax.broadcasted_iota(jnp.int32, (rows, rows), 0)
        q = lax.broadcasted_iota(jnp.int32, (rows, rows), 1)
        earlier = jnp.where((r // 8 == q // 8) & (q < r), 1.0, 0.0).astype(BF16)
        hits = jnp.broadcast_to(hit, (rows, META))
        rank = jnp.dot(earlier, hits.astype(BF16), preferred_element_type=F32)
        r = lax.broadcasted_iota(jnp.int32, (rows, META), 0)
        base = (r // 8 % 2) * 32 + (r // 128) * 16 + (r // 16 % 8) * 2
        match = (lane.astype(F32) == base.astype(F32) + rank) & (hits > 0.5)
        pick = jnp.where(match, 1.0, 0.0)
        S[xx] = jnp.transpose(pick)[:64].astype(BF16)
        give = jnp.where(match, jnp.broadcast_to(gate, (rows, META)), 0.0)
        un_ref[xx] = give.reshape(16, 16, META)[:, :8].reshape(128, META).astype(BF16)

    def pack(h, xx):
        if h == 0:
            routes(xx)
        slab = G[xx, :, :, :, cols(h)].reshape(rows, chunks[h][1])
        got = jnp.dot(S[xx], slab, preferred_element_type=F32).astype(BF16)
        R[y, xx, :, :, cols(h)] = got.reshape(2, 32, chunks[h][1])

    def packed(g, xx, ds):
        return R.at[g, xx, :, :, ds]

    def y_send(h, k, xx):
        b = packed(y, xx, cols(h))
        go(remote(b, b, ys.at[h, k, 0], yr.at[h, k, 0], dyp))
        go(remote(b, b, ys.at[h, k, 1], yr.at[h, k, 1], dym))

    def y_forward(h, k, xx):
        lo, hi = halves(h)
        b = packed(ym, xx, cols(h))
        remote(b, b, ys.at[h, k, 0], yr.at[h, k, 0], dyp).wait_recv()
        b = packed(ym, xx, lo)
        go(remote(b, b, ys.at[h, k, 2], yr.at[h, k, 2], dyp))
        b = packed(yp, xx, cols(h))
        remote(b, b, ys.at[h, k, 1], yr.at[h, k, 1], dym).wait_recv()
        b = packed(yp, xx, hi)
        go(remote(b, b, ys.at[h, k, 3], yr.at[h, k, 3], dym))

    def y_last(h, k, xx):
        lo, hi = halves(h)
        b = packed(ya, xx, lo)
        remote(b, b, ys.at[h, k, 2], yr.at[h, k, 2], dyp).wait_recv()
        b = packed(ya, xx, hi)
        remote(b, b, ys.at[h, k, 3], yr.at[h, k, 3], dym).wait_recv()

    order = [x, xm, xp, xa]

    def multiply(h):
        start, size = chunks[h]
        if h == 0:
            start, size = META, size - META
            for load in loads:
                load.wait()
        f = pl.ds(start - META, size)
        at = pl.ds(start, size)
        tok = R[:, :, 0, :, at].reshape(512, size)
        grad = R[:, :, 1, :, at].reshape(512, size)
        a = jnp.dot(tok, wg[f, :], preferred_element_type=F32)
        b = jnp.dot(tok, wu[f, :], preferred_element_type=F32)
        u = dot_nt(grad, wd[:, f])
        if h == 0:
            acc[0], acc[1], acc[2] = a, b, u
        else:
            acc[0] += a
            acc[1] += b
            acc[2] += u

    z_send(0, 0)
    for step in range(4):
        z_advance(0, step)
    x_start(0)
    waiting = []
    for h in range(nc):
        more = h + 1 < nc
        if more:
            z_send(h + 1, 0)
        shared(h, 0, x)
        pack(h, x)
        y_send(h, 0, x)
        if waiting:
            y_forward(*waiting.pop(0))
        if more:
            z_advance(h + 1, 0)
        x_forward(h)
        if more:
            z_advance(h + 1, 1)
        shared(h, 1, xm)
        pack(h, xm)
        y_send(h, 1, xm)
        y_forward(h, 0, x)
        if more:
            z_advance(h + 1, 2)
        shared(h, 2, xp)
        pack(h, xp)
        y_send(h, 2, xp)
        if more:
            z_advance(h + 1, 3)
            x_start(h + 1)
        x_last(h)
        y_forward(h, 1, xm)
        shared(h, 3, xa)
        pack(h, xa)
        y_send(h, 3, xa)
        y_forward(h, 2, xp)
        waiting.append((h, 3, xa))
        if h:
            for k, xx in enumerate(order):
                y_last(h - 1, k, xx)
            multiply(h - 1)
    y_forward(*waiting.pop(0))
    for k, xx in enumerate(order):
        y_last(nc - 1, k, xx)
    multiply(nc - 1)
    lane = lax.broadcasted_iota(jnp.int32, (128, META), 1)
    for g in range(4):
        at = pl.ds(g * 128, 128)
        a, b, u = acc[0, at, :], acc[1, at, :], acc[2, at, :]
        sig = jax.nn.sigmoid(a)
        active = a * sig
        s = jnp.sum(active * b * u, axis=1, keepdims=True)
        da_ref[at, :] = (u * b * sig * (1.0 + a * (1.0 - sig))).astype(BF16)
        db_ref[at, :] = (u * active).astype(BF16)
        meta = R[g, :, 0, :, 0:META].reshape(128, META).astype(F32)
        chosen = jnp.where(lane < 8, meta, -1.0) == e.astype(F32)
        gate = jnp.sum(jnp.where(chosen, pltpu.roll(meta, META - 8, 1), 0.0), axis=1, keepdims=True)
        sg_ref[g] = jnp.transpose(jnp.where(lane == 0, s, jnp.where(lane == 1, gate, 0.0)))[:8]
    for copy in sent:
        copy.wait_send()


def forward(blk, wg, wu, wd, pieces):
    width = blk.shape[1] - META
    step = width // pieces
    chunks = [(META + i * step, step) for i in range(pieces)]
    chunks[0] = (0, META + step)
    vm = pl.BlockSpec(memory_space=pltpu.VMEM)
    hbm = pl.BlockSpec(memory_space=pl.ANY)
    D = pltpu.SemaphoreType.DMA
    shape = jax.ShapeDtypeStruct
    return pl.pallas_call(
        functools.partial(forward_kernel, chunks),
        out_shape=(
            shape((512, 256), BF16), shape((512, 256), BF16), shape((NY, 8, META), F32),
            shape((NX, 128, META), BF16),
        ),
        in_specs=[vm, hbm, hbm, hbm],
        out_specs=(vm, vm, vm, vm),
        scratch_shapes=[
            pltpu.VMEM((NX, NC, NZ, 16, width + META), BF16),
            pltpu.VMEM((NY, NX, 2, 32, width + META), BF16),
            pltpu.VMEM((NX, 64, 256), BF16),
            pltpu.VMEM((width, 256), BF16), pltpu.VMEM((width, 256), BF16), pltpu.VMEM((256, width), BF16),
            pltpu.VMEM((3, 512, 256), F32),
            D((3,)), D((pieces, 7)), D((pieces, 7)), D((pieces, 4)), D((pieces, 4)),
            D((pieces, 4)), D((pieces, 4)), D((pieces, 4, 4)), D((pieces, 4, 4)),
        ],
        compiler_params=pltpu.CompilerParams(
            collective_id=1, has_side_effects=True, vmem_limit_bytes=60 << 20
        ),
        name="forward",
    )(blk, wg, wu, wd)


def backward_kernel(
    chunks, da, db, sg, un, wg_hbm, wu_hbm, out_ref, fis_ref,
    O, R1, R2, E, DS, RC, X1, X2, Fz, RZ, SB, wg, wu,
    lsem, ss, sr, ys, yr, cs, cr, xs, xr, zs, zr,
):
    x, z, c, y = position()
    nc = len(chunks)
    xp, xm, xa = lax.rem(x + 1, NX), lax.rem(x + NX - 1, NX), lax.rem(x + 2, NX)
    zp, zm = lax.rem(z + 1, NZ), lax.rem(z + NZ - 1, NZ)
    yp, ym, ya = lax.rem(y + 1, NY), lax.rem(y + NY - 1, NY), lax.rem(y + 2, NY)
    co = 1 - c
    dxp, dxm = place(xp, z, c, y), place(xm, z, c, y)
    dzp, dzm = place(x, zp, c, y), place(x, zm, c, y)
    dyp, dym, dya = place(x, z, c, yp), place(x, z, c, ym), place(x, z, c, ya)
    dco = place(x, z, co, y)

    def rows_of(h):
        return pl.ds(chunks[h][0], chunks[h][1])

    loads = []
    for h in range(nc):
        for i, (src, dst) in enumerate(((wg_hbm, wg), (wu_hbm, wu))):
            load = pltpu.make_async_copy(src.at[rows_of(h), :], dst.at[rows_of(h), :], lsem.at[h, i])
            load.start()
            loads.append(load)
    SB[y] = sg[...]
    meet([dxp, dxm, dzp, dzm, dyp, dym, dya, dco])
    sent = []

    def go(copy):
        copy.start()
        sent.append(copy)

    def got(dst, send, recv, device):
        remote(dst, dst, send, recv, device).wait_recv()

    score = [(dyp, ym), (dym, yp), (dya, ya)]
    for i, (device, _) in enumerate(score):
        go(remote(SB.at[y], SB.at[y], ss.at[i], sr.at[i], device))

    def halves(h):
        start, size = chunks[h]
        return pl.ds(start, size // 2), pl.ds(start + size // 2, size // 2)

    def half(h):
        start, size = chunks[h]
        return pl.ds(start // 2, size // 2)

    def up(v):
        return v.astype(F32)

    def stage_a(h):
        at = rows_of(h)
        loads[2 * h].wait()
        loads[2 * h + 1].wait()
        part = dot_nt(da[...], wg[at, :]) + dot_nt(db[...], wu[at, :])
        O[:, :, :, at] = part.astype(BF16).reshape(NY, NX, 32, chunks[h][1])
        lo, hi = halves(h)
        go(remote(O.at[ya, :, :, lo], R1.at[0, :, :, half(h)], ys.at[h, 0], yr.at[h, 0], dyp))
        go(remote(O.at[ya, :, :, hi], R1.at[1, :, :, half(h)], ys.at[h, 1], yr.at[h, 1], dym))

    def stage_b(h):
        at = rows_of(h)
        lo, hi = halves(h)
        got(R1.at[0, :, :, half(h)], ys.at[h, 0], yr.at[h, 0], dyp)
        O[yp, :, :, lo] = (up(O[yp, :, :, lo]) + up(R1[0, :, :, half(h)])).astype(BF16)
        go(remote(O.at[yp, :, :, at], R2.at[0, :, :, at], ys.at[h, 2], yr.at[h, 2], dyp))
        got(R1.at[1, :, :, half(h)], ys.at[h, 1], yr.at[h, 1], dym)
        O[ym, :, :, hi] = (up(O[ym, :, :, hi]) + up(R1[1, :, :, half(h)])).astype(BF16)
        go(remote(O.at[ym, :, :, at], R2.at[1, :, :, at], ys.at[h, 3], yr.at[h, 3], dym))

    def stage_c(h):
        at = rows_of(h)
        got(R2.at[0, :, :, at], ys.at[h, 2], yr.at[h, 2], dyp)
        got(R2.at[1, :, :, at], ys.at[h, 3], yr.at[h, 3], dym)
        for t in range(NX):
            back = (up(O[y, t, :, at]) + up(R2[0, t, :, at]) + up(R2[1, t, :, at])).astype(BF16)
            mine = un[t, pl.ds(pl.multiple_of(c * 64, 64), 64), :][:, :32]
            theirs = un[t, pl.ds(pl.multiple_of(co * 64, 64), 64), :][:, :32]
            DS[t, :, at] = jnp.dot(theirs, back, preferred_element_type=F32).astype(BF16)
            E[t, :, at] = jnp.dot(mine, back, preferred_element_type=F32).astype(BF16)
        go(remote(DS.at[:, :, at], RC.at[:, :, at], cs.at[h], cr.at[h], dco))

    def stage_d(h):
        at = rows_of(h)
        lo, hi = halves(h)
        got(RC.at[:, :, at], cs.at[h], cr.at[h], dco)
        E[:, :, at] = (up(E[:, :, at]) + up(RC[:, :, at])).astype(BF16)
        go(remote(E.at[xa, :, lo], X1.at[0, :, half(h)], xs.at[h, 0], xr.at[h, 0], dxp))
        go(remote(E.at[xa, :, hi], X1.at[1, :, half(h)], xs.at[h, 1], xr.at[h, 1], dxm))

    def stage_e(h):
        at = rows_of(h)
        lo, hi = halves(h)
        got(X1.at[0, :, half(h)], xs.at[h, 0], xr.at[h, 0], dxp)
        E[xp, :, lo] = (up(E[xp, :, lo]) + up(X1[0, :, half(h)])).astype(BF16)
        go(remote(E.at[xp, :, at], X2.at[0, :, at], xs.at[h, 2], xr.at[h, 2], dxp))
        got(X1.at[1, :, half(h)], xs.at[h, 1], xr.at[h, 1], dxm)
        E[xm, :, hi] = (up(E[xm, :, hi]) + up(X1[1, :, half(h)])).astype(BF16)
        go(remote(E.at[xm, :, at], X2.at[1, :, at], xs.at[h, 3], xr.at[h, 3], dxm))

    def zrow(off):
        return lax.rem(z + off + NZ, NZ)

    def z_send(h, step):
        at = rows_of(h)
        if step < 4:
            go(remote(Fz.at[zrow(4 - step), :, at], RZ.at[step, :, at], zs.at[h, step], zr.at[h, step], dzp))
        if step < 3:
            go(remote(Fz.at[zrow(step - 3), :, at], RZ.at[4 + step, :, at], zs.at[h, 4 + step], zr.at[h, 4 + step], dzm))

    def stage_f(h):
        at = rows_of(h)
        got(X2.at[0, :, at], xs.at[h, 2], xr.at[h, 2], dxp)
        got(X2.at[1, :, at], xs.at[h, 3], xr.at[h, 3], dxm)
        total = up(E[x, :, at]) + up(X2[0, :, at]) + up(X2[1, :, at])
        Fz[:, :, at] = total.reshape(NZ, 8, chunks[h][1])
        z_send(h, 0)

    def stage_z(step):
        def run(h):
            at = rows_of(h)
            got(RZ.at[step - 1, :, at], zs.at[h, step - 1], zr.at[h, step - 1], dzp)
            Fz[zrow(4 - step), :, at] += RZ[step - 1, :, at]
            if step < 4:
                got(RZ.at[3 + step, :, at], zs.at[h, 3 + step], zr.at[h, 3 + step], dzm)
                Fz[zrow(step - 3), :, at] += RZ[3 + step, :, at]
                if step < 3:
                    z_send(h, step)
                else:
                    go(remote(Fz.at[zrow(1), :, at], RZ.at[3, :, at], zs.at[h, 3], zr.at[h, 3], dzp))
            else:
                out_ref[:, at] = Fz[z, :, at].astype(BF16)
        return run

    stages = [stage_a, stage_b, stage_c, stage_d, stage_e, stage_f] + [stage_z(i) for i in (1, 2, 3, 4)]
    for i in range(nc + len(stages) - 1):
        for lag, stage in enumerate(stages):
            if 0 <= i - lag < nc:
                stage(i - lag)
    for i, (device, who) in enumerate(score):
        got(SB.at[who], ss.at[i], sr.at[i], device)
    dots = SB[0, :, 0, :] + SB[1, :, 0, :] + SB[2, :, 0, :] + SB[3, :, 0, :]
    fis_ref[0] = jnp.sum((sg[:, 1, :] * dots) ** 2) * (1.0 / 256.0)
    for copy in sent:
        copy.wait_send()


def backward(da, db, sg, un, wg, wu, pieces):
    width = wg.shape[0]
    step = width // pieces
    chunks = [(i * step, step) for i in range(pieces)]
    vm = pl.BlockSpec(memory_space=pltpu.VMEM)
    hbm = pl.BlockSpec(memory_space=pl.ANY)
    D = pltpu.SemaphoreType.DMA
    return pl.pallas_call(
        functools.partial(backward_kernel, chunks),
        out_shape=(jax.ShapeDtypeStruct((8, width), BF16), jax.ShapeDtypeStruct((1,), F32)),
        in_specs=[vm, vm, vm, vm, hbm, hbm],
        out_specs=(vm, pl.BlockSpec(memory_space=pltpu.SMEM)),
        scratch_shapes=[
            pltpu.VMEM((NY, NX, 32, width), BF16),
            pltpu.VMEM((2, NX, 32, width // 2), BF16),
            pltpu.VMEM((2, NX, 32, width), BF16),
            pltpu.VMEM((NX, 64, width), BF16), pltpu.VMEM((NX, 64, width), BF16), pltpu.VMEM((NX, 64, width), BF16),
            pltpu.VMEM((2, 64, width // 2), BF16),
            pltpu.VMEM((2, 64, width), BF16),
            pltpu.VMEM((NZ, 8, width), F32),
            pltpu.VMEM((7, 8, width), F32),
            pltpu.VMEM((NY, NY, 8, META), F32),
            pltpu.VMEM((width, 256), BF16), pltpu.VMEM((width, 256), BF16),
            D((pieces, 2)), D((3,)), D((3,)), D((pieces, 4)), D((pieces, 4)), D((pieces,)), D((pieces,)),
            D((pieces, 4)), D((pieces, 4)), D((pieces, 7)), D((pieces, 7)),
        ],
        compiler_params=pltpu.CompilerParams(
            collective_id=2, has_side_effects=True, vmem_limit_bytes=60 << 20
        ),
        name="backward",
    )(da, db, sg, un, wg, wu)


def per_device(tokens, out_grads, expert_ids, gates, w_gate, w_up, w_down):
    group = lax.axis_index("dp")
    ids = lax.dynamic_slice_in_dim(expert_ids, group * 8, 8, 0).astype(BF16)
    own_gates = lax.dynamic_slice_in_dim(gates, group * 8, 8, 0)
    meta = jnp.pad(jnp.concatenate([ids, own_gates], axis=1), ((0, 0), (0, META - 16)))
    blk = jnp.concatenate(
        [jnp.concatenate([meta, meta], axis=0), jnp.concatenate([tokens, out_grads], axis=0)], axis=1
    )
    da, db, sg, un = forward(blk, w_gate[0], w_up[0], w_down[0], FORWARD_PIECES)
    return backward(da, db, sg, un, w_gate[0], w_up[0], BACKWARD_PIECES)


def solution(mesh):
    placed = (
        P(("expert", "dp"), None), P(("expert", "dp"), None), P("expert", None), P("expert", None),
        P("expert", None, "dp"), P("expert", None, "dp"), P("expert", "dp", None),
    )
    return jax.shard_map(
        per_device, mesh=mesh, in_specs=placed,
        out_specs=(P(("expert", "dp"), None), P("expert")), check_vma=False,
    )
```

```python
import functools

import jax
import jax.numpy as jnp
from jax import lax
from jax.experimental import pallas as pl
from jax.experimental.pallas import tpu as pltpu
from jax.sharding import PartitionSpec as P

F32, BF16 = jnp.float32, jnp.bfloat16
NX, NZ, NC, NY = 4, 8, 2, 4
META = 128
LATE_TILES = (14, 14, 14)
EARLY_TILES = (7, 7)
LEAD = 2
EARLY_SLOTS = (1, 2, 3, 4, 5, 10, 12)
BACKWARD_PIECES = 7
MESH = pl.DeviceIdType.MESH


def position():
    e = lax.axis_index("expert")
    return lax.div(e, NZ * NC), lax.rem(lax.div(e, NC), NZ), lax.rem(e, NC), lax.axis_index("dp")


def place(x, z, c, y):
    return {"expert": (x * NZ + z) * NC + c, "dp": y}


def remote(src, dst, send, recv, device):
    return pltpu.make_async_remote_copy(
        src_ref=src, dst_ref=dst, send_sem=send, recv_sem=recv, device_id=device, device_id_type=MESH
    )


def meet(peers):
    barrier = pltpu.get_barrier_semaphore()
    for peer in peers:
        pl.semaphore_signal(barrier, inc=1, device_id=peer, device_id_type=MESH)
    pl.semaphore_wait(barrier, len(peers))


def dot_nt(left, right):
    return lax.dot_general(left, right, (((1,), (1,)), ((), ())), preferred_element_type=F32)


def forward_kernel(
    chunks, early, blk, wg_hbm, wu_hbm, wd_hbm, da_ref, db_ref, sg_ref, un_ref,
    G, H, R, S, wg, wu, wd, acc, lsem, xs, xr, zs, zr, cs, cr, ys, yr,
    ks, kr, hys, hyr, hzs, hzr, hxs, hxr, hcs, hcr,
):
    x, z, c, y = position()
    e = lax.axis_index("expert")
    nc = len(chunks)
    xp, xm, xa = lax.rem(x + 1, NX), lax.rem(x + NX - 1, NX), lax.rem(x + 2, NX)
    zp, zm = lax.rem(z + 1, NZ), lax.rem(z + NZ - 1, NZ)
    yp, ym, ya = lax.rem(y + 1, NY), lax.rem(y + NY - 1, NY), lax.rem(y + 2, NY)
    co = 1 - c
    dxp, dxm = place(xp, z, c, y), place(xm, z, c, y)
    dzp, dzm = place(x, zp, c, y), place(x, zm, c, y)
    dyp, dym = place(x, z, c, yp), place(x, z, c, ym)
    dco = place(x, z, co, y)
    dya, dxa = place(x, z, c, ya), place(xa, z, c, y)
    wide = early[0][0]
    loads = [
        pltpu.make_async_copy(wg_hbm, wg, lsem.at[0]),
        pltpu.make_async_copy(wu_hbm, wu, lsem.at[1]),
        pltpu.make_async_copy(wd_hbm, wd, lsem.at[2]),
    ]
    for load in loads:
        load.start()
    G[z, x, c] = blk[:, :wide]
    H[x, c, z, y] = blk[:, wide:]
    meet([dxp, dxm, dxa, dzp, dzm, dyp, dym, dya, dco])
    sent = []

    def go(copy):
        copy.start()
        sent.append(copy)

    def cols(h):
        return pl.ds(chunks[h][0], chunks[h][1])

    def halves(h):
        start, size = chunks[h]
        first = size // 2 // 128 * 128
        return pl.ds(start, first), pl.ds(start + first, size - first)

    others_x = [(dxp, xm), (dxm, xp), (dxa, xa)]
    others_y = [(dyp, ym), (dym, yp), (dya, ya)]
    near = [0, -1, 1, -2, 2, -3, 3, 4]
    phases = [(0,), (1, 2), (3, 4), (5, 6), (7,)]

    def turn(off):
        return lax.rem(z + off + NZ, NZ)

    def ring(block, step, arriving):
        if step < 3:
            return [
                (block(-step - arriving, pl.ds(0, 4)), step, dzp),
                (block(step + arriving, pl.ds(0, 4)), 3 + step, dzm),
            ]
        return [
            (block(-step - arriving, pl.ds(0, 2)), 6, dzp),
            (block(step + arriving, pl.ds(2, 2)), 7, dzm),
        ]

    def ring_send(block, send, recv, step):
        for b, i, device in ring(block, step, 0):
            go(remote(b, b, send(i), recv(i), device))

    def ring_wait(block, send, recv, step):
        for b, i, device in ring(block, step, 1):
            remote(b, b, send(i), recv(i), device).wait_recv()

    def late_x(h):
        b = G.at[z, x, c, :, cols(h)]
        for i, (device, _) in enumerate(others_x):
            go(remote(b, b, xs.at[h, i], xr.at[h, i], device))

    def late_block(h):
        return lambda off, part: G.at[turn(off), part, c, :, cols(h)]

    def late_share(h, i):
        b = G.at[turn(near[i]), :, c, :, cols(h)]
        go(remote(b, b, cs.at[h, i], cr.at[h, i], dco))

    def late_z(h):
        for i, (device, who) in enumerate(others_x):
            b = G.at[z, who, c, :, cols(h)]
            remote(b, b, xs.at[h, i], xr.at[h, i], device).wait_recv()
        ring_send(late_block(h), lambda i: zs.at[h, i], lambda i: zr.at[h, i], 0)
        late_share(h, 0)

    def late_advance(h, step):
        args = (late_block(h), lambda i: zs.at[h, i], lambda i: zr.at[h, i])
        ring_wait(*args, step)
        if step < 3:
            ring_send(*args, step + 1)
        for i in phases[step + 1]:
            late_share(h, i)

    rows = NX * NC * 16

    def routes(zz):
        meta = G[zz, :, :, :, 0:META].reshape(rows, META).astype(F32)
        lane = lax.broadcasted_iota(jnp.int32, (rows, META), 1)
        chosen = jnp.where(lane < 8, meta, -1.0) == e.astype(F32)
        gates = pltpu.roll(meta, META - 8, 1)
        hit = jnp.sum(chosen.astype(F32), axis=1, keepdims=True)
        gate = jnp.sum(jnp.where(chosen, gates, 0.0), axis=1, keepdims=True)
        r = lax.broadcasted_iota(jnp.int32, (rows, rows), 0)
        q = lax.broadcasted_iota(jnp.int32, (rows, rows), 1)
        earlier = jnp.where((r // 8 == q // 8) & (q < r), 1.0, 0.0).astype(BF16)
        hits = jnp.broadcast_to(hit, (rows, META))
        rank = jnp.dot(earlier, hits.astype(BF16), preferred_element_type=F32)
        slot = (r // 16 * 2).astype(F32) + rank
        lanes = lane.astype(F32)
        match = (lanes == slot + (r // 8 % 2 * 16).astype(F32)) & (hits > 0.5)
        S[y, zz] = jnp.transpose(jnp.where(match, 1.0, 0.0))[:32].astype(BF16)
        match = (lanes == slot + zz.astype(F32) * 16.0) & (hits > 0.5)
        give = jnp.where(match, jnp.broadcast_to(gate, (rows, META)), 0.0)
        un_ref[:, :, zz] = give.reshape(NX, NC, 16, META)[:, :, :8]

    def late_pack(h, i):
        zz = turn(near[i])
        b = G.at[zz, :, co, :, cols(h)]
        remote(b, b, cs.at[h, i], cr.at[h, i], dco).wait_recv()
        if h == 0:
            routes(zz)
        size = chunks[h][1]
        slab = G[zz, :, :, :, cols(h)].reshape(rows, size)
        got = jnp.dot(S[y, zz], slab, preferred_element_type=F32).astype(BF16)
        R[y, zz, :, :, cols(h)] = got.reshape(2, 16, size)
        b = R.at[y, zz, :, :, cols(h)]
        go(remote(b, b, ys.at[h, i, 0], yr.at[h, i, 0], dyp))
        go(remote(b, b, ys.at[h, i, 1], yr.at[h, i, 1], dym))

    def y_forward(h, i):
        zz = turn(near[i])
        lo, hi = halves(h)
        b = R.at[ym, zz, :, :, cols(h)]
        remote(b, b, ys.at[h, i, 0], yr.at[h, i, 0], dyp).wait_recv()
        b = R.at[ym, zz, :, :, lo]
        go(remote(b, b, ys.at[h, i, 2], yr.at[h, i, 2], dyp))
        b = R.at[yp, zz, :, :, cols(h)]
        remote(b, b, ys.at[h, i, 1], yr.at[h, i, 1], dym).wait_recv()
        b = R.at[yp, zz, :, :, hi]
        go(remote(b, b, ys.at[h, i, 3], yr.at[h, i, 3], dym))

    def y_last(h):
        lo, hi = halves(h)
        for i in range(NZ):
            zz = turn(near[i])
            b = R.at[ya, zz, :, :, lo]
            remote(b, b, ys.at[h, i, 2], yr.at[h, i, 2], dyp).wait_recv()
            b = R.at[ya, zz, :, :, hi]
            remote(b, b, ys.at[h, i, 3], yr.at[h, i, 3], dym).wait_recv()

    def multiply(start, size):
        if start == 0:
            start, size = META, size - META
            for load in loads:
                load.wait()
            acc[...] = jnp.zeros_like(acc)
        f = pl.ds(start - META, size)
        at = pl.ds(start, size)
        tok = R[:, :, 0, :, at].reshape(512, size)
        grad = R[:, :, 1, :, at].reshape(512, size)
        acc[0] += jnp.dot(tok, wg[f, :], preferred_element_type=F32)
        acc[1] += jnp.dot(tok, wu[f, :], preferred_element_type=F32)
        acc[2] += dot_nt(grad, wd[:, f])

    def own(q):
        return pl.ds(early[q][0] - wide, early[q][1])

    def early_y(q):
        b = H.at[x, c, z, y, :, own(q)]
        for i, (device, _) in enumerate(others_y):
            go(remote(b, b, hys.at[q, i], hyr.at[q, i], device))

    def early_block(q):
        return lambda off, part: H.at[x, c, turn(off), part, :, own(q)]

    def early_z(q):
        for i, (device, who) in enumerate(others_y):
            b = H.at[x, c, z, who, :, own(q)]
            remote(b, b, hys.at[q, i], hyr.at[q, i], device).wait_recv()
        ring_send(early_block(q), lambda i: hzs.at[q, i], lambda i: hzr.at[q, i], 0)

    def early_advance(q, step):
        args = (early_block(q), lambda i: hzs.at[q, i], lambda i: hzr.at[q, i])
        ring_wait(*args, step)
        if step < 3:
            ring_send(*args, step + 1)
        else:
            b = early_line(q, x, c)
            go(remote(b, b, hxs.at[q, 0], hxr.at[q, 0], dxp))
            go(remote(b, b, hxs.at[q, 1], hxr.at[q, 1], dxm))
            early_share(q, 0, x)

    def early_line(q, xx, cc, part=slice(None)):
        return H.at[xx, cc, part, :, :, own(q)]

    def early_share(q, i, xx):
        b = early_line(q, xx, c)
        go(remote(b, b, hcs.at[q, i], hcr.at[q, i], dco))

    def early_forward(q):
        for i, who, part, device in ((0, xm, pl.ds(0, 4), dxp), (1, xp, pl.ds(4, 4), dxm)):
            b = early_line(q, who, c)
            remote(b, b, hxs.at[q, i], hxr.at[q, i], device).wait_recv()
            b = early_line(q, who, c, part)
            go(remote(b, b, hxs.at[q, 2 + i], hxr.at[q, 2 + i], device))
            early_share(q, 1 + i, who)

    def early_last(q):
        for i, part, device in ((2, pl.ds(0, 4), dxp), (3, pl.ds(4, 4), dxm)):
            b = early_line(q, xa, c, part)
            remote(b, b, hxs.at[q, i], hxr.at[q, i], device).wait_recv()
        early_share(q, 3, xa)

    def early_pack(q):
        for i, who in enumerate((x, xm, xp, xa)):
            b = early_line(q, who, co)
            remote(b, b, hcs.at[q, i], hcr.at[q, i], dco).wait_recv()
        start, size = early[q]

        def body(i, carry):
            g, zz = lax.div(i, NZ), lax.rem(i, NZ)
            slab = H[:, :, zz, g, :, own(q)].reshape(rows, size)
            got = jnp.dot(S[g, zz], slab, preferred_element_type=F32).astype(BF16)
            R[g, zz, :, :, pl.ds(start, size)] = got.reshape(2, 16, size)
            return carry

        lax.fori_loop(0, NY * NZ, body, 0)

    nq = len(early)
    todo = [[functools.partial(early_z, q) for q in range(nq)]]
    todo += [[functools.partial(early_advance, q, step) for q in range(nq)] for step in range(4)]
    todo += [[functools.partial(early_forward, q)] for q in range(nq)]
    slots = list(EARLY_SLOTS)

    late_x(0)
    for q in range(nq):
        early_y(q)
    for h in range(1, nc):
        late_x(h)
    late_z(0)
    ahead = []
    for h in range(nc):
        for step in range(-1, 4):
            ahead.append((max(0, 5 * h + step + 1 - (LEAD if h else 0)), h, step))
    ahead = [item for item in ahead if item[1:] != (0, -1)]
    ready = []
    for slot in range(5 * nc):
        h, p = divmod(slot, 5)
        while ahead and ahead[0][0] <= slot:
            _, hh, step = ahead.pop(0)
            if step < 0:
                late_z(hh)
            else:
                late_advance(hh, step)
        for i in phases[p]:
            late_pack(h, i)
        while ready:
            y_forward(*ready.pop(0))
        ready = [(h, i) for i in phases[p]]
        if slot == 4:
            for i, (device, _) in enumerate(others_y):
                go(remote(S.at[y], S.at[y], ks.at[i], kr.at[i], device))
        while slots and slots[0] <= slot:
            slots.pop(0)
            for event in todo.pop(0):
                event()
        if h and p == 2:
            y_last(h - 1)
            multiply(*chunks[h - 1])
    while ready:
        y_forward(*ready.pop(0))
    while todo:
        for event in todo.pop(0):
            event()
    for q in range(nq):
        early_last(q)
    for i, (device, who) in enumerate(others_y):
        remote(S.at[who], S.at[who], ks.at[i], kr.at[i], device).wait_recv()
    for q in range(nq):
        early_pack(q)
        multiply(*early[q])
    y_last(nc - 1)
    multiply(*chunks[nc - 1])
    lane = lax.broadcasted_iota(jnp.int32, (128, META), 1)
    for g in range(4):
        at = pl.ds(g * 128, 128)
        a, b, u = acc[0, at, :], acc[1, at, :], acc[2, at, :]
        sig = jax.nn.sigmoid(a)
        active = a * sig
        s = jnp.sum(active * b * u, axis=1, keepdims=True)
        da_ref[at, :] = (u * b * sig * (1.0 + a * (1.0 - sig))).astype(BF16)
        db_ref[at, :] = (u * active).astype(BF16)
        meta = R[g, :, 0, :, 0:META].reshape(128, META).astype(F32)
        chosen = jnp.where(lane < 8, meta, -1.0) == e.astype(F32)
        gate = jnp.sum(jnp.where(chosen, pltpu.roll(meta, META - 8, 1), 0.0), axis=1, keepdims=True)
        sg_ref[g] = jnp.transpose(jnp.where(lane == 0, s, jnp.where(lane == 1, gate, 0.0)))[:8]
    for copy in sent:
        copy.wait_send()


def forward(blk, wg, wu, wd):
    width = blk.shape[1] - META
    chunks, start = [], 0
    for tiles in LATE_TILES + EARLY_TILES:
        size = tiles * 128 + (0 if start else META)
        chunks.append((start, size))
        start += size
    pieces, nq = len(LATE_TILES), len(EARLY_TILES)
    chunks, early = chunks[:pieces], chunks[pieces:]
    wide = early[0][0]
    vm = pl.BlockSpec(memory_space=pltpu.VMEM)
    hbm = pl.BlockSpec(memory_space=pl.ANY)
    D = pltpu.SemaphoreType.DMA
    shape = jax.ShapeDtypeStruct
    return pl.pallas_call(
        functools.partial(forward_kernel, chunks, early),
        out_shape=(
            shape((512, 256), BF16), shape((512, 256), BF16), shape((NY, 8, META), F32),
            shape((NX, NC, NZ, 8, META), F32),
        ),
        in_specs=[vm, hbm, hbm, hbm],
        out_specs=(vm, vm, vm, vm),
        scratch_shapes=[
            pltpu.VMEM((NZ, NX, NC, 16, wide), BF16),
            pltpu.VMEM((NX, NC, NZ, NY, 16, width + META - wide), BF16),
            pltpu.VMEM((NY, NZ, 2, 16, width + META), BF16),
            pltpu.VMEM((NY, NZ, 32, 128), BF16),
            pltpu.VMEM((width, 256), BF16), pltpu.VMEM((width, 256), BF16), pltpu.VMEM((256, width), BF16),
            pltpu.VMEM((3, 512, 256), F32),
            D((3,)), D((pieces, 3)), D((pieces, 3)), D((pieces, 8)), D((pieces, 8)),
            D((pieces, 8)), D((pieces, 8)), D((pieces, 8, 4)), D((pieces, 8, 4)),
            D((3,)), D((3,)), D((nq, 3)), D((nq, 3)), D((nq, 8)), D((nq, 8)),
            D((nq, 4)), D((nq, 4)), D((nq, 4)), D((nq, 4)),
        ],
        compiler_params=pltpu.CompilerParams(
            collective_id=1, has_side_effects=True, vmem_limit_bytes=60 << 20
        ),
        name="forward",
    )(blk, wg, wu, wd)


def backward_kernel(
    chunks, da, db, sg, un, wg_hbm, wu_hbm, out_ref, fis_ref,
    O, R1, R2, E, DS, RC, X1, X2, Fz, RZ, SB, wg, wu,
    lsem, ss, sr, ys, yr, cs, cr, xs, xr, zs, zr,
):
    x, z, c, y = position()
    nc = len(chunks)
    xp, xm, xa = lax.rem(x + 1, NX), lax.rem(x + NX - 1, NX), lax.rem(x + 2, NX)
    zp, zm = lax.rem(z + 1, NZ), lax.rem(z + NZ - 1, NZ)
    yp, ym, ya = lax.rem(y + 1, NY), lax.rem(y + NY - 1, NY), lax.rem(y + 2, NY)
    co = 1 - c
    dxp, dxm = place(xp, z, c, y), place(xm, z, c, y)
    dzp, dzm = place(x, zp, c, y), place(x, zm, c, y)
    dyp, dym, dya = place(x, z, c, yp), place(x, z, c, ym), place(x, z, c, ya)
    dco = place(x, z, co, y)

    def rows_of(h):
        return pl.ds(chunks[h][0], chunks[h][1])

    loads = []
    for h in range(nc):
        for i, (src, dst) in enumerate(((wg_hbm, wg), (wu_hbm, wu))):
            load = pltpu.make_async_copy(src.at[rows_of(h), :], dst.at[rows_of(h), :], lsem.at[h, i])
            load.start()
            loads.append(load)
    SB[y] = sg[...]
    meet([dxp, dxm, dzp, dzm, dyp, dym, dya, dco])
    sent = []

    def go(copy):
        copy.start()
        sent.append(copy)

    def got(dst, send, recv, device):
        remote(dst, dst, send, recv, device).wait_recv()

    score = [(dyp, ym), (dym, yp), (dya, ya)]
    for i, (device, _) in enumerate(score):
        go(remote(SB.at[y], SB.at[y], ss.at[i], sr.at[i], device))

    def halves(h):
        start, size = chunks[h]
        return pl.ds(start, size // 2), pl.ds(start + size // 2, size // 2)

    def half(h):
        start, size = chunks[h]
        return pl.ds(start // 2, size // 2)

    def up(v):
        return v.astype(F32)

    def stage_a(h):
        at = rows_of(h)
        loads[2 * h].wait()
        loads[2 * h + 1].wait()
        part = dot_nt(da[...], wg[at, :]) + dot_nt(db[...], wu[at, :])
        O[:, :, at] = part.astype(BF16).reshape(NY, 128, chunks[h][1])
        lo, hi = halves(h)
        go(remote(O.at[ya, :, lo], R1.at[0, :, half(h)], ys.at[h, 0], yr.at[h, 0], dyp))
        go(remote(O.at[ya, :, hi], R1.at[1, :, half(h)], ys.at[h, 1], yr.at[h, 1], dym))

    def stage_b(h):
        at = rows_of(h)
        lo, hi = halves(h)
        got(R1.at[0, :, half(h)], ys.at[h, 0], yr.at[h, 0], dyp)
        O[yp, :, lo] = (up(O[yp, :, lo]) + up(R1[0, :, half(h)])).astype(BF16)
        go(remote(O.at[yp, :, at], R2.at[0, :, at], ys.at[h, 2], yr.at[h, 2], dyp))
        got(R1.at[1, :, half(h)], ys.at[h, 1], yr.at[h, 1], dym)
        O[ym, :, hi] = (up(O[ym, :, hi]) + up(R1[1, :, half(h)])).astype(BF16)
        go(remote(O.at[ym, :, at], R2.at[1, :, at], ys.at[h, 3], yr.at[h, 3], dym))

    def stage_c(h):
        at = rows_of(h)
        got(R2.at[0, :, at], ys.at[h, 2], yr.at[h, 2], dyp)
        got(R2.at[1, :, at], ys.at[h, 3], yr.at[h, 3], dym)
        back = (up(O[y, :, at]) + up(R2[0, :, at]) + up(R2[1, :, at])).astype(BF16)
        for t in range(NX):
            mine = un[t, c].reshape(64, META).astype(BF16)
            theirs = un[t, co].reshape(64, META).astype(BF16)
            DS[t, :, at] = jnp.dot(theirs, back, preferred_element_type=F32).astype(BF16)
            E[t, :, at] = jnp.dot(mine, back, preferred_element_type=F32).astype(BF16)
        go(remote(DS.at[:, :, at], RC.at[:, :, at], cs.at[h], cr.at[h], dco))

    def stage_d(h):
        at = rows_of(h)
        lo, hi = halves(h)
        got(RC.at[:, :, at], cs.at[h], cr.at[h], dco)
        E[:, :, at] = (up(E[:, :, at]) + up(RC[:, :, at])).astype(BF16)
        go(remote(E.at[xa, :, lo], X1.at[0, :, half(h)], xs.at[h, 0], xr.at[h, 0], dxp))
        go(remote(E.at[xa, :, hi], X1.at[1, :, half(h)], xs.at[h, 1], xr.at[h, 1], dxm))

    def stage_e(h):
        at = rows_of(h)
        lo, hi = halves(h)
        got(X1.at[0, :, half(h)], xs.at[h, 0], xr.at[h, 0], dxp)
        E[xp, :, lo] = (up(E[xp, :, lo]) + up(X1[0, :, half(h)])).astype(BF16)
        go(remote(E.at[xp, :, at], X2.at[0, :, at], xs.at[h, 2], xr.at[h, 2], dxp))
        got(X1.at[1, :, half(h)], xs.at[h, 1], xr.at[h, 1], dxm)
        E[xm, :, hi] = (up(E[xm, :, hi]) + up(X1[1, :, half(h)])).astype(BF16)
        go(remote(E.at[xm, :, at], X2.at[1, :, at], xs.at[h, 3], xr.at[h, 3], dxm))

    def zrow(off):
        return lax.rem(z + off + NZ, NZ)

    def z_send(h, step):
        at = rows_of(h)
        if step < 4:
            go(remote(Fz.at[zrow(4 - step), :, at], RZ.at[step, :, at], zs.at[h, step], zr.at[h, step], dzp))
        if step < 3:
            go(remote(Fz.at[zrow(step - 3), :, at], RZ.at[4 + step, :, at], zs.at[h, 4 + step], zr.at[h, 4 + step], dzm))

    def stage_f(h):
        at = rows_of(h)
        got(X2.at[0, :, at], xs.at[h, 2], xr.at[h, 2], dxp)
        got(X2.at[1, :, at], xs.at[h, 3], xr.at[h, 3], dxm)
        total = up(E[x, :, at]) + up(X2[0, :, at]) + up(X2[1, :, at])
        Fz[:, :, at] = total.reshape(NZ, 8, chunks[h][1])
        z_send(h, 0)

    def stage_z(step):
        def run(h):
            at = rows_of(h)
            got(RZ.at[step - 1, :, at], zs.at[h, step - 1], zr.at[h, step - 1], dzp)
            Fz[zrow(4 - step), :, at] += RZ[step - 1, :, at]
            if step < 4:
                got(RZ.at[3 + step, :, at], zs.at[h, 3 + step], zr.at[h, 3 + step], dzm)
                Fz[zrow(step - 3), :, at] += RZ[3 + step, :, at]
                if step < 3:
                    z_send(h, step)
                else:
                    go(remote(Fz.at[zrow(1), :, at], RZ.at[3, :, at], zs.at[h, 3], zr.at[h, 3], dzp))
            else:
                out_ref[:, at] = Fz[z, :, at].astype(BF16)
        return run

    stages = [stage_a, stage_b, stage_c, stage_d, stage_e, stage_f] + [stage_z(i) for i in (1, 2, 3, 4)]
    for i in range(nc + len(stages) - 1):
        for lag, stage in enumerate(stages):
            if 0 <= i - lag < nc:
                stage(i - lag)
    for i, (device, who) in enumerate(score):
        got(SB.at[who], ss.at[i], sr.at[i], device)
    dots = SB[0, :, 0, :] + SB[1, :, 0, :] + SB[2, :, 0, :] + SB[3, :, 0, :]
    fis_ref[0] = jnp.sum((sg[:, 1, :] * dots) ** 2) * (1.0 / 256.0)
    for copy in sent:
        copy.wait_send()


def backward(da, db, sg, un, wg, wu, pieces):
    width = wg.shape[0]
    step = width // pieces
    chunks = [(i * step, step) for i in range(pieces)]
    vm = pl.BlockSpec(memory_space=pltpu.VMEM)
    hbm = pl.BlockSpec(memory_space=pl.ANY)
    D = pltpu.SemaphoreType.DMA
    return pl.pallas_call(
        functools.partial(backward_kernel, chunks),
        out_shape=(jax.ShapeDtypeStruct((8, width), BF16), jax.ShapeDtypeStruct((1,), F32)),
        in_specs=[vm, vm, vm, vm, hbm, hbm],
        out_specs=(vm, pl.BlockSpec(memory_space=pltpu.SMEM)),
        scratch_shapes=[
            pltpu.VMEM((NY, 128, width), BF16),
            pltpu.VMEM((2, 128, width // 2), BF16),
            pltpu.VMEM((2, 128, width), BF16),
            pltpu.VMEM((NX, 64, width), BF16), pltpu.VMEM((NX, 64, width), BF16), pltpu.VMEM((NX, 64, width), BF16),
            pltpu.VMEM((2, 64, width // 2), BF16),
            pltpu.VMEM((2, 64, width), BF16),
            pltpu.VMEM((NZ, 8, width), F32),
            pltpu.VMEM((7, 8, width), F32),
            pltpu.VMEM((NY, NY, 8, META), F32),
            pltpu.VMEM((width, 256), BF16), pltpu.VMEM((width, 256), BF16),
            D((pieces, 2)), D((3,)), D((3,)), D((pieces, 4)), D((pieces, 4)), D((pieces,)), D((pieces,)),
            D((pieces, 4)), D((pieces, 4)), D((pieces, 7)), D((pieces, 7)),
        ],
        compiler_params=pltpu.CompilerParams(
            collective_id=2, has_side_effects=True, vmem_limit_bytes=60 << 20
        ),
        name="backward",
    )(da, db, sg, un, wg, wu)


def per_device(tokens, out_grads, expert_ids, gates, w_gate, w_up, w_down):
    group = lax.axis_index("dp")
    ids = lax.dynamic_slice_in_dim(expert_ids, group * 8, 8, 0).astype(BF16)
    own_gates = lax.dynamic_slice_in_dim(gates, group * 8, 8, 0)
    meta = jnp.pad(jnp.concatenate([ids, own_gates], axis=1), ((0, 0), (0, META - 16)))
    blk = jnp.concatenate(
        [jnp.concatenate([meta, meta], axis=0), jnp.concatenate([tokens, out_grads], axis=0)], axis=1
    )
    da, db, sg, un = forward(blk, w_gate[0], w_up[0], w_down[0])
    return backward(da, db, sg, un, w_gate[0], w_up[0], BACKWARD_PIECES)


def solution(mesh):
    placed = (
        P(("expert", "dp"), None), P(("expert", "dp"), None), P("expert", None), P("expert", None),
        P("expert", None, "dp"), P("expert", None, "dp"), P("expert", "dp", None),
    )
    return jax.shard_map(
        per_device, mesh=mesh, in_specs=placed,
        out_specs=(P(("expert", "dp"), None), P("expert")), check_vma=False,
    )
```

```python
import functools

import jax
import jax.numpy as jnp
from jax import lax
from jax.experimental import pallas as pl
from jax.experimental.pallas import tpu as pltpu
from jax.sharding import PartitionSpec as P

F32, BF16 = jnp.float32, jnp.bfloat16
NX, NZ, NC, NY = 4, 8, 2, 4
META = 128
LATE_TILES = (16, 18, 10)
EARLY_TILES = (12,)
LEAD, LAG = 1, 2
EARLY_SLOTS = (0, 1, 2, 3, 4, 9, 13, 14)
BACKWARD_TILES = (8,) * 7
BACKWARD_LAGS = (0, 2, 4, 5, 6, 7)
MESH = pl.DeviceIdType.MESH


def position():
    e = lax.axis_index("expert")
    return lax.div(e, NZ * NC), lax.rem(lax.div(e, NC), NZ), lax.rem(e, NC), lax.axis_index("dp")


def place(x, z, c, y):
    return {"expert": (x * NZ + z) * NC + c, "dp": y}


def remote(src, dst, send, recv, device):
    return pltpu.make_async_remote_copy(
        src_ref=src, dst_ref=dst, send_sem=send, recv_sem=recv, device_id=device, device_id_type=MESH
    )


def meet(peers):
    barrier = pltpu.get_barrier_semaphore()
    for peer in peers:
        pl.semaphore_signal(barrier, inc=1, device_id=peer, device_id_type=MESH)
    pl.semaphore_wait(barrier, len(peers))


def dot_nt(left, right):
    return lax.dot_general(left, right, (((1,), (1,)), ((), ())), preferred_element_type=F32)


def forward_kernel(
    chunks, early, blk, wg_hbm, wu_hbm, wd_hbm, da_ref, db_ref, sg_ref, un_ref,
    G, H, R, S, wg, wu, wd, acc, lsem, xs, xr, zs, zr, cs, cr, ys, yr,
    ks, kr, hys, hyr, hzs, hzr, hxs, hxr, hcs, hcr,
):
    x, z, c, y = position()
    e = lax.axis_index("expert")
    nc = len(chunks)
    xp, xm, xa = lax.rem(x + 1, NX), lax.rem(x + NX - 1, NX), lax.rem(x + 2, NX)
    zp, zm = lax.rem(z + 1, NZ), lax.rem(z + NZ - 1, NZ)
    yp, ym, ya = lax.rem(y + 1, NY), lax.rem(y + NY - 1, NY), lax.rem(y + 2, NY)
    co = 1 - c
    dxp, dxm = place(xp, z, c, y), place(xm, z, c, y)
    dzp, dzm = place(x, zp, c, y), place(x, zm, c, y)
    dyp, dym = place(x, z, c, yp), place(x, z, c, ym)
    dco = place(x, z, co, y)
    dya, dxa = place(x, z, c, ya), place(xa, z, c, y)
    wide = early[0][0]
    loads = [
        pltpu.make_async_copy(wg_hbm, wg, lsem.at[0]),
        pltpu.make_async_copy(wu_hbm, wu, lsem.at[1]),
        pltpu.make_async_copy(wd_hbm, wd, lsem.at[2]),
    ]
    for load in loads:
        load.start()
    G[z, x, c] = blk[:, :wide]
    H[x, c, z, y] = blk[:, wide:]
    meet([dxp, dxm, dxa, dzp, dzm, dyp, dym, dya, dco])
    sent = []

    def go(copy):
        copy.start()
        sent.append(copy)

    def cols(h):
        return pl.ds(chunks[h][0], chunks[h][1])

    def halves(h):
        start, size = chunks[h]
        first = size // 2 // 128 * 128
        return pl.ds(start, first), pl.ds(start + first, size - first)

    others_x = [(dxp, xm), (dxm, xp), (dxa, xa)]
    others_y = [(dyp, ym), (dym, yp), (dya, ya)]
    near = [0, -1, 1, -2, 2, -3, 3, 4]
    phases = [(0,), (1, 2), (3, 4), (5, 6), (7,)]

    def turn(off):
        return lax.rem(z + off + NZ, NZ)

    def ring(block, step, arriving):
        if step < 3:
            return [
                (block(-step - arriving, pl.ds(0, 4)), step, dzp),
                (block(step + arriving, pl.ds(0, 4)), 3 + step, dzm),
            ]
        return [
            (block(-step - arriving, pl.ds(0, 2)), 6, dzp),
            (block(step + arriving, pl.ds(2, 2)), 7, dzm),
        ]

    def ring_send(block, send, recv, step):
        for b, i, device in ring(block, step, 0):
            go(remote(b, b, send(i), recv(i), device))

    def ring_wait(block, send, recv, step):
        for b, i, device in ring(block, step, 1):
            remote(b, b, send(i), recv(i), device).wait_recv()

    def late_x(h):
        b = G.at[z, x, c, :, cols(h)]
        for i, (device, _) in enumerate(others_x):
            go(remote(b, b, xs.at[h, i], xr.at[h, i], device))

    def late_block(h):
        return lambda off, part: G.at[turn(off), part, c, :, cols(h)]

    def late_share(h, i):
        b = G.at[turn(near[i]), :, c, :, cols(h)]
        go(remote(b, b, cs.at[h, i], cr.at[h, i], dco))

    def late_near(h):
        for i, (device, who) in enumerate(others_x):
            b = G.at[z, who, c, :, cols(h)]
            remote(b, b, xs.at[h, i], xr.at[h, i], device).wait_recv()
        late_share(h, 0)

    def late_z(h):
        ring_send(late_block(h), lambda i: zs.at[h, i], lambda i: zr.at[h, i], 0)

    def late_advance(h, step):
        args = (late_block(h), lambda i: zs.at[h, i], lambda i: zr.at[h, i])
        ring_wait(*args, step)
        if step < 3:
            ring_send(*args, step + 1)
        for i in phases[step + 1]:
            late_share(h, i)

    rows = NX * NC * 16

    def routes(zz):
        meta = G[zz, :, :, :, 0:META].reshape(rows, META).astype(F32)
        lane = lax.broadcasted_iota(jnp.int32, (rows, META), 1)
        chosen = jnp.where(lane < 8, meta, -1.0) == e.astype(F32)
        gates = pltpu.roll(meta, META - 8, 1)
        hit = jnp.sum(chosen.astype(F32), axis=1, keepdims=True)
        gate = jnp.sum(jnp.where(chosen, gates, 0.0), axis=1, keepdims=True)
        r = lax.broadcasted_iota(jnp.int32, (rows, rows), 0)
        q = lax.broadcasted_iota(jnp.int32, (rows, rows), 1)
        earlier = jnp.where((r // 8 == q // 8) & (q < r), 1.0, 0.0).astype(BF16)
        hits = jnp.broadcast_to(hit, (rows, META))
        rank = jnp.dot(earlier, hits.astype(BF16), preferred_element_type=F32)
        slot = (r // 16 * 2).astype(F32) + rank
        lanes = lane.astype(F32)
        match = (lanes == slot + (r // 8 % 2 * 16).astype(F32)) & (hits > 0.5)
        S[y, zz] = jnp.transpose(jnp.where(match, 1.0, 0.0))[:32].astype(BF16)
        match = (lanes == slot + zz.astype(F32) * 16.0) & (hits > 0.5)
        give = jnp.where(match, jnp.broadcast_to(gate, (rows, META)), 0.0)
        un_ref[:, :, zz] = give.reshape(NX, NC, 16, META)[:, :, :8]

    def late_pack(h, i):
        zz = turn(near[i])
        b = G.at[zz, :, co, :, cols(h)]
        remote(b, b, cs.at[h, i], cr.at[h, i], dco).wait_recv()
        if h == 0:
            routes(zz)
        size = chunks[h][1]
        slab = G[zz, :, :, :, cols(h)].reshape(rows, size)
        got = jnp.dot(S[y, zz], slab, preferred_element_type=F32).astype(BF16)
        R[y, zz, :, :, cols(h)] = got.reshape(2, 16, size)
        b = R.at[y, zz, :, :, cols(h)]
        go(remote(b, b, ys.at[h, i, 0], yr.at[h, i, 0], dyp))
        go(remote(b, b, ys.at[h, i, 1], yr.at[h, i, 1], dym))

    def y_forward(h, i):
        zz = turn(near[i])
        lo, hi = halves(h)
        b = R.at[ym, zz, :, :, cols(h)]
        remote(b, b, ys.at[h, i, 0], yr.at[h, i, 0], dyp).wait_recv()
        b = R.at[ym, zz, :, :, lo]
        go(remote(b, b, ys.at[h, i, 2], yr.at[h, i, 2], dyp))
        b = R.at[yp, zz, :, :, cols(h)]
        remote(b, b, ys.at[h, i, 1], yr.at[h, i, 1], dym).wait_recv()
        b = R.at[yp, zz, :, :, hi]
        go(remote(b, b, ys.at[h, i, 3], yr.at[h, i, 3], dym))

    def y_last(h):
        lo, hi = halves(h)
        for i in range(NZ):
            zz = turn(near[i])
            b = R.at[ya, zz, :, :, lo]
            remote(b, b, ys.at[h, i, 2], yr.at[h, i, 2], dyp).wait_recv()
            b = R.at[ya, zz, :, :, hi]
            remote(b, b, ys.at[h, i, 3], yr.at[h, i, 3], dym).wait_recv()

    def multiply(start, size):
        if start == 0:
            start, size = META, size - META
            for load in loads:
                load.wait()
            acc[...] = jnp.zeros_like(acc)
        f = pl.ds(start - META, size)
        at = pl.ds(start, size)
        tok = R[:, :, 0, :, at].reshape(512, size)
        grad = R[:, :, 1, :, at].reshape(512, size)
        acc[0] += jnp.dot(tok, wg[f, :], preferred_element_type=F32)
        acc[1] += jnp.dot(tok, wu[f, :], preferred_element_type=F32)
        acc[2] += dot_nt(grad, wd[:, f])

    def own(q):
        return pl.ds(early[q][0] - wide, early[q][1])

    def early_y(q):
        b = H.at[x, c, z, y, :, own(q)]
        for i, (device, _) in enumerate(others_y):
            go(remote(b, b, hys.at[q, i], hyr.at[q, i], device))

    def early_block(q):
        return lambda off, part: H.at[x, c, turn(off), part, :, own(q)]

    def early_z(q):
        for i, (device, who) in enumerate(others_y):
            b = H.at[x, c, z, who, :, own(q)]
            remote(b, b, hys.at[q, i], hyr.at[q, i], device).wait_recv()
        ring_send(early_block(q), lambda i: hzs.at[q, i], lambda i: hzr.at[q, i], 0)

    def early_advance(q, step):
        args = (early_block(q), lambda i: hzs.at[q, i], lambda i: hzr.at[q, i])
        ring_wait(*args, step)
        if step < 3:
            ring_send(*args, step + 1)
        else:
            b = early_line(q, x, c)
            go(remote(b, b, hxs.at[q, 0], hxr.at[q, 0], dxp))
            go(remote(b, b, hxs.at[q, 1], hxr.at[q, 1], dxm))
            early_share(q, 0, x)

    def early_line(q, xx, cc, part=slice(None)):
        return H.at[xx, cc, part, :, :, own(q)]

    def early_share(q, i, xx):
        b = early_line(q, xx, c)
        go(remote(b, b, hcs.at[q, i], hcr.at[q, i], dco))

    def early_forward(q):
        for i, who, part, device in ((0, xm, pl.ds(0, 4), dxp), (1, xp, pl.ds(4, 4), dxm)):
            b = early_line(q, who, c)
            remote(b, b, hxs.at[q, i], hxr.at[q, i], device).wait_recv()
            b = early_line(q, who, c, part)
            go(remote(b, b, hxs.at[q, 2 + i], hxr.at[q, 2 + i], device))
            early_share(q, 1 + i, who)

    def early_last(q):
        for i, part, device in ((2, pl.ds(0, 4), dxp), (3, pl.ds(4, 4), dxm)):
            b = early_line(q, xa, c, part)
            remote(b, b, hxs.at[q, i], hxr.at[q, i], device).wait_recv()
        early_share(q, 3, xa)

    def early_pack(q):
        for i, who in enumerate((x, xm, xp, xa)):
            b = early_line(q, who, co)
            remote(b, b, hcs.at[q, i], hcr.at[q, i], dco).wait_recv()
        start, size = early[q]

        def body(i, carry):
            g, zz = lax.div(i, NZ), lax.rem(i, NZ)
            slab = H[:, :, zz, g, :, own(q)].reshape(rows, size)
            got = jnp.dot(S[g, zz], slab, preferred_element_type=F32).astype(BF16)
            R[g, zz, :, :, pl.ds(start, size)] = got.reshape(2, 16, size)
            return carry

        lax.fori_loop(0, NY * NZ, body, 0)

    def early_finish(q):
        if q == 0:
            for i, (device, who) in enumerate(others_y):
                remote(S.at[who], S.at[who], ks.at[i], kr.at[i], device).wait_recv()
        early_pack(q)
        multiply(*early[q])

    nq = len(early)
    todo = [[functools.partial(early_z, q) for q in range(nq)]]
    todo += [[functools.partial(early_advance, q, step) for q in range(nq)] for step in range(4)]
    todo += [[functools.partial(early_forward, q)] for q in range(nq)]
    todo += [[functools.partial(early_last, q)] for q in range(nq)]
    todo += [[functools.partial(early_finish, q)] for q in range(nq)]
    slots = list(EARLY_SLOTS)

    late_x(0)
    for q in range(nq):
        early_y(q)
    for h in range(1, nc):
        late_x(h)
    while slots and slots[0] < 0:
        slots.pop(0)
        for event in todo.pop(0):
            event()
    late_near(0)
    late_z(0)
    for h in range(1, nc):
        late_near(h)
    ahead = []
    for h in range(nc):
        for step in range(-1, 4):
            ahead.append((max(0, 5 * h + step + 1 - (LEAD if h else 0)), h, step))
    ahead = [item for item in ahead if item[1:] != (0, -1)]
    ready = []

    def forward_until(slot):
        while ready and ready[0][0] <= slot:
            y_forward(*ready.pop(0)[1:])

    for slot in range(5 * nc):
        h, p = divmod(slot, 5)
        while ahead and ahead[0][0] <= slot:
            _, hh, step = ahead.pop(0)
            if step < 0:
                late_z(hh)
            else:
                late_advance(hh, step)
        now = [(hh, 0) for hh in range(nc)] if slot == 0 else [(h, i) for i in phases[p] if i]
        for item in now:
            late_pack(*item)
        forward_until(slot - LAG)
        ready += [(slot, *item) for item in now]
        if slot == 4:
            for i, (device, _) in enumerate(others_y):
                go(remote(S.at[y], S.at[y], ks.at[i], kr.at[i], device))
        while slots and slots[0] <= slot:
            slots.pop(0)
            for event in todo.pop(0):
                event()
        if h and p == 2:
            forward_until(5 * h - 1)
            y_last(h - 1)
            multiply(*chunks[h - 1])
    forward_until(5 * nc)
    while todo:
        for event in todo.pop(0):
            event()
    y_last(nc - 1)
    multiply(*chunks[nc - 1])
    lane = lax.broadcasted_iota(jnp.int32, (128, META), 1)
    for g in range(4):
        at = pl.ds(g * 128, 128)
        a, b, u = acc[0, at, :], acc[1, at, :], acc[2, at, :]
        sig = jax.nn.sigmoid(a)
        active = a * sig
        s = jnp.sum(active * b * u, axis=1, keepdims=True)
        da_ref[at, :] = (u * b * sig * (1.0 + a * (1.0 - sig))).astype(BF16)
        db_ref[at, :] = (u * active).astype(BF16)
        meta = R[g, :, 0, :, 0:META].reshape(128, META).astype(F32)
        chosen = jnp.where(lane < 8, meta, -1.0) == e.astype(F32)
        gate = jnp.sum(jnp.where(chosen, pltpu.roll(meta, META - 8, 1), 0.0), axis=1, keepdims=True)
        sg_ref[g] = jnp.transpose(jnp.where(lane == 0, s, jnp.where(lane == 1, gate, 0.0)))[:8]
    for copy in sent:
        copy.wait_send()


def forward(blk, wg, wu, wd):
    width = blk.shape[1] - META
    chunks, start = [], 0
    for tiles in LATE_TILES + EARLY_TILES:
        size = tiles * 128 + (0 if start else META)
        chunks.append((start, size))
        start += size
    pieces, nq = len(LATE_TILES), len(EARLY_TILES)
    chunks, early = chunks[:pieces], chunks[pieces:]
    wide = early[0][0]
    vm = pl.BlockSpec(memory_space=pltpu.VMEM)
    hbm = pl.BlockSpec(memory_space=pl.ANY)
    D = pltpu.SemaphoreType.DMA
    shape = jax.ShapeDtypeStruct
    return pl.pallas_call(
        functools.partial(forward_kernel, chunks, early),
        out_shape=(
            shape((512, 256), BF16), shape((512, 256), BF16), shape((NY, 8, META), F32),
            shape((NX, NC, NZ, 8, META), F32),
        ),
        in_specs=[vm, hbm, hbm, hbm],
        out_specs=(vm, vm, vm, vm),
        scratch_shapes=[
            pltpu.VMEM((NZ, NX, NC, 16, wide), BF16),
            pltpu.VMEM((NX, NC, NZ, NY, 16, width + META - wide), BF16),
            pltpu.VMEM((NY, NZ, 2, 16, width + META), BF16),
            pltpu.VMEM((NY, NZ, 32, 128), BF16),
            pltpu.VMEM((width, 256), BF16), pltpu.VMEM((width, 256), BF16), pltpu.VMEM((256, width), BF16),
            pltpu.VMEM((3, 512, 256), F32),
            D((3,)), D((pieces, 3)), D((pieces, 3)), D((pieces, 8)), D((pieces, 8)),
            D((pieces, 8)), D((pieces, 8)), D((pieces, 8, 4)), D((pieces, 8, 4)),
            D((3,)), D((3,)), D((nq, 3)), D((nq, 3)), D((nq, 8)), D((nq, 8)),
            D((nq, 4)), D((nq, 4)), D((nq, 4)), D((nq, 4)),
        ],
        compiler_params=pltpu.CompilerParams(
            collective_id=1, has_side_effects=True, vmem_limit_bytes=60 << 20
        ),
        name="forward",
    )(blk, wg, wu, wd)


def backward_kernel(
    chunks, da, db, sg, un, wg_hbm, wu_hbm, out_ref, fis_ref,
    O, R1, R2, E, DS, RC, X, Fz, RZ, SB, wg, wu,
    lsem, ss, sr, ys, yr, cs, cr, xs, xr, zs, zr,
):
    x, z, c, y = position()
    nc = len(chunks)
    xp, xm, xa = lax.rem(x + 1, NX), lax.rem(x + NX - 1, NX), lax.rem(x + 2, NX)
    yp, ym, ya = lax.rem(y + 1, NY), lax.rem(y + NY - 1, NY), lax.rem(y + 2, NY)
    co = 1 - c
    dxp, dxm, dxa = place(xp, z, c, y), place(xm, z, c, y), place(xa, z, c, y)
    reach = (1, -1, 2, -2, 3, -3, 4)

    def turn(off):
        return lax.rem(z + off + NZ, NZ)

    dyp, dym, dya = place(x, z, c, yp), place(x, z, c, ym), place(x, z, c, ya)
    dco = place(x, z, co, y)

    def rows_of(h):
        return pl.ds(chunks[h][0], chunks[h][1])

    loads = []
    for h in range(nc):
        for i, (src, dst) in enumerate(((wg_hbm, wg), (wu_hbm, wu))):
            load = pltpu.make_async_copy(src.at[rows_of(h), :], dst.at[rows_of(h), :], lsem.at[h, i])
            load.start()
            loads.append(load)
    SB[y] = sg[...]
    meet([dxp, dxm, dxa, dyp, dym, dya, dco] + [place(x, turn(off), c, y) for off in reach])
    sent = []

    def go(copy):
        copy.start()
        sent.append(copy)

    def got(dst, send, recv, device):
        remote(dst, dst, send, recv, device).wait_recv()

    score = [(dyp, ym), (dym, yp), (dya, ya)]
    for i, (device, _) in enumerate(score):
        go(remote(SB.at[y], SB.at[y], ss.at[i], sr.at[i], device))

    def halves(h):
        start, size = chunks[h]
        return pl.ds(start, size // 2), pl.ds(start + size // 2, size // 2)

    def half(h):
        start, size = chunks[h]
        return pl.ds(start // 2, size // 2)

    def up(v):
        return v.astype(F32)

    def stage_a(h):
        at = rows_of(h)
        loads[2 * h].wait()
        loads[2 * h + 1].wait()
        part = dot_nt(da[...], wg[at, :]) + dot_nt(db[...], wu[at, :])
        O[:, :, at] = part.astype(BF16).reshape(NY, 128, chunks[h][1])
        lo, hi = halves(h)
        go(remote(O.at[ya, :, lo], R1.at[0, :, half(h)], ys.at[h, 0], yr.at[h, 0], dyp))
        go(remote(O.at[ya, :, hi], R1.at[1, :, half(h)], ys.at[h, 1], yr.at[h, 1], dym))

    def stage_b(h):
        at = rows_of(h)
        lo, hi = halves(h)
        got(R1.at[0, :, half(h)], ys.at[h, 0], yr.at[h, 0], dyp)
        O[yp, :, lo] = (up(O[yp, :, lo]) + up(R1[0, :, half(h)])).astype(BF16)
        go(remote(O.at[yp, :, at], R2.at[0, :, at], ys.at[h, 2], yr.at[h, 2], dyp))
        got(R1.at[1, :, half(h)], ys.at[h, 1], yr.at[h, 1], dym)
        O[ym, :, hi] = (up(O[ym, :, hi]) + up(R1[1, :, half(h)])).astype(BF16)
        go(remote(O.at[ym, :, at], R2.at[1, :, at], ys.at[h, 3], yr.at[h, 3], dym))

    def stage_c(h):
        at = rows_of(h)
        got(R2.at[0, :, at], ys.at[h, 2], yr.at[h, 2], dyp)
        got(R2.at[1, :, at], ys.at[h, 3], yr.at[h, 3], dym)
        back = (up(O[y, :, at]) + up(R2[0, :, at]) + up(R2[1, :, at])).astype(BF16)
        for t in range(NX):
            mine = un[t, c].reshape(64, META).astype(BF16)
            theirs = un[t, co].reshape(64, META).astype(BF16)
            DS[t, :, at] = jnp.dot(theirs, back, preferred_element_type=F32).astype(BF16)
            E[t, :, at] = jnp.dot(mine, back, preferred_element_type=F32).astype(BF16)
        go(remote(DS.at[:, :, at], RC.at[:, :, at], cs.at[h], cr.at[h], dco))

    def stage_d(h):
        at = rows_of(h)
        got(RC.at[:, :, at], cs.at[h], cr.at[h], dco)
        E[:, :, at] = (up(E[:, :, at]) + up(RC[:, :, at])).astype(BF16)
        for i, (who, device) in enumerate(((xp, dxp), (xm, dxm), (xa, dxa))):
            go(remote(E.at[who, :, at], X.at[i, :, at], xs.at[h, i], xr.at[h, i], device))

    def stage_e(h):
        at = rows_of(h)
        total = up(E[x, :, at])
        for i in range(3):
            got(X.at[i, :, at], xs.at[h, i], xr.at[h, i], dxp)
            total += up(X[i, :, at])
        size = chunks[h][1]
        total = total.reshape(NZ, 8, size)
        total = jnp.concatenate([total[:, :, : size // 2], total[:, :, size // 2 :]], axis=1)
        Fz[:, :, half(h)] = total.astype(BF16)
        for i, off in enumerate(reach):
            src = Fz.at[turn(off), :, half(h)]
            go(remote(src, RZ.at[i, :, half(h)], zs.at[h, i], zr.at[h, i], place(x, turn(off), c, y)))

    def stage_f(h):
        lo, hi = halves(h)
        total = up(Fz[z, :, half(h)])
        for i in range(7):
            got(RZ.at[i, :, half(h)], zs.at[h, i], zr.at[h, i], dxp)
            total += up(RZ[i, :, half(h)])
        out_ref[:, lo] = total[:8].astype(BF16)
        out_ref[:, hi] = total[8:].astype(BF16)

    stages = [stage_a, stage_b, stage_c, stage_d, stage_e, stage_f]
    for i in range(nc + BACKWARD_LAGS[-1]):
        for lag, stage in zip(BACKWARD_LAGS, stages):
            if 0 <= i - lag < nc:
                stage(i - lag)
    for i, (device, who) in enumerate(score):
        got(SB.at[who], ss.at[i], sr.at[i], device)
    dots = SB[0, :, 0, :] + SB[1, :, 0, :] + SB[2, :, 0, :] + SB[3, :, 0, :]
    fis_ref[0] = jnp.sum((sg[:, 1, :] * dots) ** 2) * (1.0 / 256.0)
    for copy in sent:
        copy.wait_send()


def backward(da, db, sg, un, wg, wu):
    width = wg.shape[0]
    chunks, start = [], 0
    for tiles in BACKWARD_TILES:
        chunks.append((start, tiles * 128))
        start += tiles * 128
    pieces = len(chunks)
    vm = pl.BlockSpec(memory_space=pltpu.VMEM)
    hbm = pl.BlockSpec(memory_space=pl.ANY)
    D = pltpu.SemaphoreType.DMA
    return pl.pallas_call(
        functools.partial(backward_kernel, chunks),
        out_shape=(jax.ShapeDtypeStruct((8, width), BF16), jax.ShapeDtypeStruct((1,), F32)),
        in_specs=[vm, vm, vm, vm, hbm, hbm],
        out_specs=(vm, pl.BlockSpec(memory_space=pltpu.SMEM)),
        scratch_shapes=[
            pltpu.VMEM((NY, 128, width), BF16),
            pltpu.VMEM((2, 128, width // 2), BF16),
            pltpu.VMEM((2, 128, width), BF16),
            pltpu.VMEM((NX, 64, width), BF16), pltpu.VMEM((NX, 64, width), BF16), pltpu.VMEM((NX, 64, width), BF16),
            pltpu.VMEM((3, 64, width), BF16),
            pltpu.VMEM((NZ, 16, width // 2), BF16),
            pltpu.VMEM((7, 16, width // 2), BF16),
            pltpu.VMEM((NY, NY, 8, META), F32),
            pltpu.VMEM((width, 256), BF16), pltpu.VMEM((width, 256), BF16),
            D((pieces, 2)), D((3,)), D((3,)), D((pieces, 4)), D((pieces, 4)), D((pieces,)), D((pieces,)),
            D((pieces, 3)), D((pieces, 3)), D((pieces, 7)), D((pieces, 7)),
        ],
        compiler_params=pltpu.CompilerParams(
            collective_id=2, has_side_effects=True, vmem_limit_bytes=60 << 20
        ),
        name="backward",
    )(da, db, sg, un, wg, wu)


def per_device(tokens, out_grads, expert_ids, gates, w_gate, w_up, w_down):
    group = lax.axis_index("dp")
    ids = lax.dynamic_slice_in_dim(expert_ids, group * 8, 8, 0).astype(BF16)
    own_gates = lax.dynamic_slice_in_dim(gates, group * 8, 8, 0)
    meta = jnp.pad(jnp.concatenate([ids, own_gates], axis=1), ((0, 0), (0, META - 16)))
    blk = jnp.concatenate(
        [jnp.concatenate([meta, meta], axis=0), jnp.concatenate([tokens, out_grads], axis=0)], axis=1
    )
    da, db, sg, un = forward(blk, w_gate[0], w_up[0], w_down[0])
    return backward(da, db, sg, un, w_gate[0], w_up[0])


def solution(mesh):
    placed = (
        P(("expert", "dp"), None), P(("expert", "dp"), None), P("expert", None), P("expert", None),
        P("expert", None, "dp"), P("expert", None, "dp"), P("expert", "dp", None),
    )
    return jax.shard_map(
        per_device, mesh=mesh, in_specs=placed,
        out_specs=(P(("expert", "dp"), None), P("expert")), check_vma=False,
    )
```

```python
import functools

import jax
import jax.numpy as jnp
from jax import lax
from jax.experimental import pallas as pl
from jax.experimental.pallas import tpu as pltpu
from jax.sharding import PartitionSpec as P

F32, BF16 = jnp.float32, jnp.bfloat16
NX, NZ, NC, NY = 4, 8, 2, 4
META = 128
LATE_TILES = (14, 18, 14)
EARLY_TILES = (10,)
LEAD, LAG = 1, 2
EARLY_SLOTS = (1, 2, 3, 4, 5, 9, 12, 13, 14, 99)
MUL = 3
BACKWARD_TILES = (8,) * 7
BACKWARD_LAGS = (0, 2, 3, 3, 4, 5)
BACKWARD_ORDER = (1, 2, 3, 4, 5, 0)
MESH = pl.DeviceIdType.MESH


def position():
    e = lax.axis_index("expert")
    return lax.div(e, NZ * NC), lax.rem(lax.div(e, NC), NZ), lax.rem(e, NC), lax.axis_index("dp")


def place(x, z, c, y):
    return {"expert": (x * NZ + z) * NC + c, "dp": y}


def remote(src, dst, send, recv, device):
    return pltpu.make_async_remote_copy(
        src_ref=src, dst_ref=dst, send_sem=send, recv_sem=recv, device_id=device, device_id_type=MESH
    )


def meet(peers):
    barrier = pltpu.get_barrier_semaphore()
    for peer in peers:
        pl.semaphore_signal(barrier, inc=1, device_id=peer, device_id_type=MESH)
    pl.semaphore_wait(barrier, len(peers))


def dot_nt(left, right):
    return lax.dot_general(left, right, (((1,), (1,)), ((), ())), preferred_element_type=F32)


def forward_kernel(
    chunks, early, blk, wg_hbm, wu_hbm, wd_hbm, da_ref, db_ref, sg_ref, un_ref,
    G, H, R, S, wg, wu, wd, acc, lsem, xs, xr, zs, zr, cs, cr, ys, yr,
    ks, kr, hys, hyr, hzs, hzr, hxs, hxr, hcs, hcr,
):
    x, z, c, y = position()
    e = lax.axis_index("expert")
    nc = len(chunks)
    xp, xm, xa = lax.rem(x + 1, NX), lax.rem(x + NX - 1, NX), lax.rem(x + 2, NX)
    zp, zm = lax.rem(z + 1, NZ), lax.rem(z + NZ - 1, NZ)
    yp, ym, ya = lax.rem(y + 1, NY), lax.rem(y + NY - 1, NY), lax.rem(y + 2, NY)
    co = 1 - c
    dxp, dxm = place(xp, z, c, y), place(xm, z, c, y)
    dzp, dzm = place(x, zp, c, y), place(x, zm, c, y)
    dyp, dym = place(x, z, c, yp), place(x, z, c, ym)
    dco = place(x, z, co, y)
    dya, dxa = place(x, z, c, ya), place(xa, z, c, y)
    wide = early[0][0]
    loads = [
        pltpu.make_async_copy(wg_hbm, wg, lsem.at[0]),
        pltpu.make_async_copy(wu_hbm, wu, lsem.at[1]),
        pltpu.make_async_copy(wd_hbm, wd, lsem.at[2]),
    ]
    for load in loads:
        load.start()
    G[z, x, c] = blk[:, :wide]
    H[x, c, z, y] = blk[:, wide:]
    meet([dxp, dxm, dxa, dzp, dzm, dyp, dym, dya, dco])
    sent = []

    def go(copy):
        copy.start()
        sent.append(copy)

    def cols(h):
        return pl.ds(chunks[h][0], chunks[h][1])

    def halves(h):
        start, size = chunks[h]
        first = size // 2 // 128 * 128
        return pl.ds(start, first), pl.ds(start + first, size - first)

    others_x = [(dxp, xm), (dxm, xp), (dxa, xa)]
    others_y = [(dyp, ym), (dym, yp), (dya, ya)]
    near = [0, -1, 1, -2, 2, -3, 3, 4]
    phases = [(0,), (1, 2), (3, 4), (5, 6), (7,)]

    def turn(off):
        return lax.rem(z + off + NZ, NZ)

    def ring(block, step, arriving):
        if step < 3:
            return [
                (block(-step - arriving, pl.ds(0, 4)), step, dzp),
                (block(step + arriving, pl.ds(0, 4)), 3 + step, dzm),
            ]
        return [
            (block(-step - arriving, pl.ds(0, 2)), 6, dzp),
            (block(step + arriving, pl.ds(2, 2)), 7, dzm),
        ]

    def ring_send(block, send, recv, step):
        for b, i, device in ring(block, step, 0):
            go(remote(b, b, send(i), recv(i), device))

    def ring_wait(block, send, recv, step):
        for b, i, device in ring(block, step, 1):
            remote(b, b, send(i), recv(i), device).wait_recv()

    def late_x(h):
        b = G.at[z, x, c, :, cols(h)]
        for i, (device, _) in enumerate(others_x):
            go(remote(b, b, xs.at[h, i], xr.at[h, i], device))

    def late_block(h):
        return lambda off, part: G.at[turn(off), part, c, :, cols(h)]

    def late_share(h, i):
        b = G.at[turn(near[i]), :, c, :, cols(h)]
        go(remote(b, b, cs.at[h, i], cr.at[h, i], dco))

    def late_near(h):
        for i, (device, who) in enumerate(others_x):
            b = G.at[z, who, c, :, cols(h)]
            remote(b, b, xs.at[h, i], xr.at[h, i], device).wait_recv()
        late_share(h, 0)

    def late_z(h):
        ring_send(late_block(h), lambda i: zs.at[h, i], lambda i: zr.at[h, i], 0)

    def late_advance(h, step):
        args = (late_block(h), lambda i: zs.at[h, i], lambda i: zr.at[h, i])
        ring_wait(*args, step)
        if step < 3:
            ring_send(*args, step + 1)
        for i in phases[step + 1]:
            late_share(h, i)

    rows = NX * NC * 16

    def routes(zz):
        meta = G[zz, :, :, :, 0:META].reshape(rows, META).astype(F32)
        lane = lax.broadcasted_iota(jnp.int32, (rows, META), 1)
        chosen = jnp.where(lane < 8, meta, -1.0) == e.astype(F32)
        gates = pltpu.roll(meta, META - 8, 1)
        hit = jnp.sum(chosen.astype(F32), axis=1, keepdims=True)
        gate = jnp.sum(jnp.where(chosen, gates, 0.0), axis=1, keepdims=True)
        r = lax.broadcasted_iota(jnp.int32, (rows, rows), 0)
        q = lax.broadcasted_iota(jnp.int32, (rows, rows), 1)
        earlier = jnp.where((r // 8 == q // 8) & (q < r), 1.0, 0.0).astype(BF16)
        hits = jnp.broadcast_to(hit, (rows, META))
        rank = jnp.dot(earlier, hits.astype(BF16), preferred_element_type=F32)
        slot = (r // 16 * 2).astype(F32) + rank
        lanes = lane.astype(F32)
        match = (lanes == slot + (r // 8 % 2 * 16).astype(F32)) & (hits > 0.5)
        S[y, zz] = jnp.transpose(jnp.where(match, 1.0, 0.0))[:32].astype(BF16)
        match = (lanes == slot + zz.astype(F32) * 16.0) & (hits > 0.5)
        give = jnp.where(match, jnp.broadcast_to(gate, (rows, META)), 0.0)
        un_ref[:, :, zz] = give.reshape(NX, NC, 16, META)[:, :, :8]

    def late_pack(h, i):
        zz = turn(near[i])
        b = G.at[zz, :, co, :, cols(h)]
        remote(b, b, cs.at[h, i], cr.at[h, i], dco).wait_recv()
        if h == 0:
            routes(zz)
        size = chunks[h][1]
        slab = G[zz, :, :, :, cols(h)].reshape(rows, size)
        got = jnp.dot(S[y, zz], slab, preferred_element_type=F32).astype(BF16)
        R[y, zz, :, :, cols(h)] = got.reshape(2, 16, size)
        b = R.at[y, zz, :, :, cols(h)]
        go(remote(b, b, ys.at[h, i, 0], yr.at[h, i, 0], dyp))
        go(remote(b, b, ys.at[h, i, 1], yr.at[h, i, 1], dym))

    def y_forward(h, i):
        zz = turn(near[i])
        lo, hi = halves(h)
        b = R.at[ym, zz, :, :, cols(h)]
        remote(b, b, ys.at[h, i, 0], yr.at[h, i, 0], dyp).wait_recv()
        b = R.at[ym, zz, :, :, lo]
        go(remote(b, b, ys.at[h, i, 2], yr.at[h, i, 2], dyp))
        b = R.at[yp, zz, :, :, cols(h)]
        remote(b, b, ys.at[h, i, 1], yr.at[h, i, 1], dym).wait_recv()
        b = R.at[yp, zz, :, :, hi]
        go(remote(b, b, ys.at[h, i, 3], yr.at[h, i, 3], dym))

    def y_last(h):
        lo, hi = halves(h)
        for i in range(NZ):
            zz = turn(near[i])
            b = R.at[ya, zz, :, :, lo]
            remote(b, b, ys.at[h, i, 2], yr.at[h, i, 2], dyp).wait_recv()
            b = R.at[ya, zz, :, :, hi]
            remote(b, b, ys.at[h, i, 3], yr.at[h, i, 3], dym).wait_recv()

    def multiply(start, size):
        if start == 0:
            start, size = META, size - META
            for load in loads:
                load.wait()
            acc[...] = jnp.zeros_like(acc)
        f = pl.ds(start - META, size)
        at = pl.ds(start, size)
        tok = R[:, :, 0, :, at].reshape(512, size)
        grad = R[:, :, 1, :, at].reshape(512, size)
        acc[0] += jnp.dot(tok, wg[f, :], preferred_element_type=F32)
        acc[1] += jnp.dot(tok, wu[f, :], preferred_element_type=F32)
        acc[2] += dot_nt(grad, wd[:, f])

    def own(q):
        return pl.ds(early[q][0] - wide, early[q][1])

    def early_y(q):
        b = H.at[x, c, z, y, :, own(q)]
        for i, (device, _) in enumerate(others_y):
            go(remote(b, b, hys.at[q, i], hyr.at[q, i], device))

    def early_block(q):
        return lambda off, part: H.at[x, c, turn(off), part, :, own(q)]

    def early_z(q):
        for i, (device, who) in enumerate(others_y):
            b = H.at[x, c, z, who, :, own(q)]
            remote(b, b, hys.at[q, i], hyr.at[q, i], device).wait_recv()
        ring_send(early_block(q), lambda i: hzs.at[q, i], lambda i: hzr.at[q, i], 0)

    def early_advance(q, step):
        args = (early_block(q), lambda i: hzs.at[q, i], lambda i: hzr.at[q, i])
        ring_wait(*args, step)
        if step < 3:
            ring_send(*args, step + 1)
        else:
            b = early_line(q, x, c)
            go(remote(b, b, hxs.at[q, 0], hxr.at[q, 0], dxp))
            go(remote(b, b, hxs.at[q, 1], hxr.at[q, 1], dxm))
            early_share(q, 0, x)

    def early_line(q, xx, cc, part=slice(None)):
        return H.at[xx, cc, part, :, :, own(q)]

    def early_share(q, i, xx):
        b = early_line(q, xx, c)
        go(remote(b, b, hcs.at[q, i], hcr.at[q, i], dco))

    def early_forward(q):
        for i, who, part, device in ((0, xm, pl.ds(0, 4), dxp), (1, xp, pl.ds(4, 4), dxm)):
            b = early_line(q, who, c)
            remote(b, b, hxs.at[q, i], hxr.at[q, i], device).wait_recv()
            b = early_line(q, who, c, part)
            go(remote(b, b, hxs.at[q, 2 + i], hxr.at[q, 2 + i], device))
            early_share(q, 1 + i, who)

    def early_last(q):
        for i, part, device in ((2, pl.ds(0, 4), dxp), (3, pl.ds(4, 4), dxm)):
            b = early_line(q, xa, c, part)
            remote(b, b, hxs.at[q, i], hxr.at[q, i], device).wait_recv()
        early_share(q, 3, xa)

    def early_arrived(q):
        for i, who in enumerate((x, xm, xp, xa)):
            b = early_line(q, who, co)
            remote(b, b, hcs.at[q, i], hcr.at[q, i], dco).wait_recv()

    def early_pack(q, some):
        if some == 0:
            early_arrived(q)
        start, size = early[q]

        def body(i, carry):
            g, zz = lax.div(i, NZ), lax.rem(i, NZ)
            slab = H[:, :, zz, g, :, own(q)].reshape(rows, size)
            got = jnp.dot(S[g, zz], slab, preferred_element_type=F32).astype(BF16)
            R[g, zz, :, :, pl.ds(start, size)] = got.reshape(2, 16, size)
            return carry

        lax.fori_loop(some * 16, some * 16 + 16, body, 0)

    def picks_arrived():
        for i, (device, who) in enumerate(others_y):
            remote(S.at[who], S.at[who], ks.at[i], kr.at[i], device).wait_recv()

    nq = len(early)
    todo = [[functools.partial(early_z, q) for q in range(nq)]]
    todo += [[functools.partial(early_advance, q, step) for q in range(nq)] for step in range(4)]
    todo += [[functools.partial(early_forward, q)] for q in range(nq)]
    todo += [[functools.partial(early_last, q)] for q in range(nq)]
    todo[-1].append(picks_arrived)
    todo += [[functools.partial(early_pack, q, some) for q in range(nq)] for some in (0, 1)]
    todo += [[functools.partial(multiply, *early[q]) for q in range(nq)]]
    slots = list(EARLY_SLOTS)

    late_x(0)
    for q in range(nq):
        early_y(q)
    for h in range(1, nc):
        late_x(h)
    while slots and slots[0] < 0:
        slots.pop(0)
        for event in todo.pop(0):
            event()
    late_near(0)
    late_z(0)
    for h in range(1, nc):
        late_near(h)
    ahead = []
    for h in range(nc):
        for step in range(-1, 4):
            ahead.append((max(0, 5 * h + step + 1 - (LEAD if h else 0)), h, step))
    ahead = [item for item in ahead if item[1:] != (0, -1)]
    ready = []

    def forward_until(slot):
        while ready and ready[0][0] <= slot:
            y_forward(*ready.pop(0)[1:])

    for slot in range(5 * nc):
        h, p = divmod(slot, 5)
        while ahead and ahead[0][0] <= slot:
            _, hh, step = ahead.pop(0)
            if step < 0:
                late_z(hh)
            else:
                late_advance(hh, step)
        now = [(hh, 0) for hh in range(nc)] if slot == 0 else [(h, i) for i in phases[p] if i]
        for item in now:
            late_pack(*item)
        forward_until(slot - LAG)
        ready += [(slot, *item) for item in now]
        if slot == 4:
            for i, (device, _) in enumerate(others_y):
                go(remote(S.at[y], S.at[y], ks.at[i], kr.at[i], device))
        while slots and slots[0] <= slot:
            slots.pop(0)
            for event in todo.pop(0):
                event()
        if h and p == MUL:
            forward_until(5 * h - 1)
            y_last(h - 1)
            multiply(*chunks[h - 1])
    forward_until(5 * nc)
    while todo:
        for event in todo.pop(0):
            event()
    y_last(nc - 1)
    multiply(*chunks[nc - 1])
    lane = lax.broadcasted_iota(jnp.int32, (128, META), 1)
    for g in range(4):
        at = pl.ds(g * 128, 128)
        a, b, u = acc[0, at, :], acc[1, at, :], acc[2, at, :]
        sig = jax.nn.sigmoid(a)
        active = a * sig
        s = jnp.sum(active * b * u, axis=1, keepdims=True)
        da_ref[at, :] = (u * b * sig * (1.0 + a * (1.0 - sig))).astype(BF16)
        db_ref[at, :] = (u * active).astype(BF16)
        meta = R[g, :, 0, :, 0:META].reshape(128, META).astype(F32)
        chosen = jnp.where(lane < 8, meta, -1.0) == e.astype(F32)
        gate = jnp.sum(jnp.where(chosen, pltpu.roll(meta, META - 8, 1), 0.0), axis=1, keepdims=True)
        sg_ref[g] = jnp.transpose(jnp.where(lane == 0, s, jnp.where(lane == 1, gate, 0.0)))[:8]
    for copy in sent:
        copy.wait_send()


def forward(blk, wg, wu, wd):
    width = blk.shape[1] - META
    chunks, start = [], 0
    for tiles in LATE_TILES + EARLY_TILES:
        size = tiles * 128 + (0 if start else META)
        chunks.append((start, size))
        start += size
    pieces, nq = len(LATE_TILES), len(EARLY_TILES)
    chunks, early = chunks[:pieces], chunks[pieces:]
    wide = early[0][0]
    vm = pl.BlockSpec(memory_space=pltpu.VMEM)
    hbm = pl.BlockSpec(memory_space=pl.ANY)
    D = pltpu.SemaphoreType.DMA
    shape = jax.ShapeDtypeStruct
    return pl.pallas_call(
        functools.partial(forward_kernel, chunks, early),
        out_shape=(
            shape((512, 256), BF16), shape((512, 256), BF16), shape((NY, 8, META), F32),
            shape((NX, NC, NZ, 8, META), F32),
        ),
        in_specs=[vm, hbm, hbm, hbm],
        out_specs=(vm, vm, vm, vm),
        scratch_shapes=[
            pltpu.VMEM((NZ, NX, NC, 16, wide), BF16),
            pltpu.VMEM((NX, NC, NZ, NY, 16, width + META - wide), BF16),
            pltpu.VMEM((NY, NZ, 2, 16, width + META), BF16),
            pltpu.VMEM((NY, NZ, 32, 128), BF16),
            pltpu.VMEM((width, 256), BF16), pltpu.VMEM((width, 256), BF16), pltpu.VMEM((256, width), BF16),
            pltpu.VMEM((3, 512, 256), F32),
            D((3,)), D((pieces, 3)), D((pieces, 3)), D((pieces, 8)), D((pieces, 8)),
            D((pieces, 8)), D((pieces, 8)), D((pieces, 8, 4)), D((pieces, 8, 4)),
            D((3,)), D((3,)), D((nq, 3)), D((nq, 3)), D((nq, 8)), D((nq, 8)),
            D((nq, 4)), D((nq, 4)), D((nq, 4)), D((nq, 4)),
        ],
        compiler_params=pltpu.CompilerParams(
            collective_id=1, has_side_effects=True, vmem_limit_bytes=60 << 20
        ),
        name="forward",
    )(blk, wg, wu, wd)


def backward_kernel(
    chunks, da, db, sg, un, wg_hbm, wu_hbm, out_ref, fis_ref,
    O, R1, R2, E, DS, RC, X, Fz, RZ, SB, wg, wu,
    lsem, ss, sr, ys, yr, cs, cr, xs, xr, zs, zr,
):
    x, z, c, y = position()
    nc = len(chunks)
    xp, xm, xa = lax.rem(x + 1, NX), lax.rem(x + NX - 1, NX), lax.rem(x + 2, NX)
    yp, ym, ya = lax.rem(y + 1, NY), lax.rem(y + NY - 1, NY), lax.rem(y + 2, NY)
    co = 1 - c
    dxp, dxm, dxa = place(xp, z, c, y), place(xm, z, c, y), place(xa, z, c, y)
    reach = (1, -1, 2, -2, 3, -3, 4)

    def turn(off):
        return lax.rem(z + off + NZ, NZ)

    dyp, dym, dya = place(x, z, c, yp), place(x, z, c, ym), place(x, z, c, ya)
    dco = place(x, z, co, y)

    def rows_of(h):
        return pl.ds(chunks[h][0], chunks[h][1])

    loads = []
    for h in range(nc):
        for i, (src, dst) in enumerate(((wg_hbm, wg), (wu_hbm, wu))):
            load = pltpu.make_async_copy(src.at[rows_of(h), :], dst.at[rows_of(h), :], lsem.at[h, i])
            load.start()
            loads.append(load)
    SB[y] = sg[...]
    meet([dxp, dxm, dxa, dyp, dym, dya, dco] + [place(x, turn(off), c, y) for off in reach])
    sent = []

    def go(copy):
        copy.start()
        sent.append(copy)

    def got(dst, send, recv, device):
        remote(dst, dst, send, recv, device).wait_recv()

    score = [(dyp, ym), (dym, yp), (dya, ya)]
    for i, (device, _) in enumerate(score):
        go(remote(SB.at[y], SB.at[y], ss.at[i], sr.at[i], device))

    def halves(h):
        start, size = chunks[h]
        return pl.ds(start, size // 2), pl.ds(start + size // 2, size // 2)

    def half(h):
        start, size = chunks[h]
        return pl.ds(start // 2, size // 2)

    def up(v):
        return v.astype(F32)

    def stage_a(h):
        at = rows_of(h)
        loads[2 * h].wait()
        loads[2 * h + 1].wait()
        part = dot_nt(da[...], wg[at, :]) + dot_nt(db[...], wu[at, :])
        O[:, :, at] = part.astype(BF16).reshape(NY, 128, chunks[h][1])
        lo, hi = halves(h)
        go(remote(O.at[ya, :, lo], R1.at[0, :, half(h)], ys.at[h, 0], yr.at[h, 0], dyp))
        go(remote(O.at[ya, :, hi], R1.at[1, :, half(h)], ys.at[h, 1], yr.at[h, 1], dym))

    def stage_b(h):
        at = rows_of(h)
        lo, hi = halves(h)
        got(R1.at[0, :, half(h)], ys.at[h, 0], yr.at[h, 0], dyp)
        O[yp, :, lo] = (up(O[yp, :, lo]) + up(R1[0, :, half(h)])).astype(BF16)
        go(remote(O.at[yp, :, at], R2.at[0, :, at], ys.at[h, 2], yr.at[h, 2], dyp))
        got(R1.at[1, :, half(h)], ys.at[h, 1], yr.at[h, 1], dym)
        O[ym, :, hi] = (up(O[ym, :, hi]) + up(R1[1, :, half(h)])).astype(BF16)
        go(remote(O.at[ym, :, at], R2.at[1, :, at], ys.at[h, 3], yr.at[h, 3], dym))

    def stage_c(h):
        at = rows_of(h)
        got(R2.at[0, :, at], ys.at[h, 2], yr.at[h, 2], dyp)
        got(R2.at[1, :, at], ys.at[h, 3], yr.at[h, 3], dym)
        back = (up(O[y, :, at]) + up(R2[0, :, at]) + up(R2[1, :, at])).astype(BF16)
        for t in range(NX):
            mine = un[t, c].reshape(64, META).astype(BF16)
            theirs = un[t, co].reshape(64, META).astype(BF16)
            DS[t, :, at] = jnp.dot(theirs, back, preferred_element_type=F32).astype(BF16)
            E[t, :, at] = jnp.dot(mine, back, preferred_element_type=F32).astype(BF16)
        go(remote(DS.at[:, :, at], RC.at[:, :, at], cs.at[h], cr.at[h], dco))

    def stage_d(h):
        at = rows_of(h)
        got(RC.at[:, :, at], cs.at[h], cr.at[h], dco)
        E[:, :, at] = (up(E[:, :, at]) + up(RC[:, :, at])).astype(BF16)
        for i, (who, device) in enumerate(((xp, dxp), (xm, dxm), (xa, dxa))):
            go(remote(E.at[who, :, at], X.at[i, :, at], xs.at[h, i], xr.at[h, i], device))

    def stage_e(h):
        at = rows_of(h)
        total = up(E[x, :, at])
        for i in range(3):
            got(X.at[i, :, at], xs.at[h, i], xr.at[h, i], dxp)
            total += up(X[i, :, at])
        size = chunks[h][1]
        total = total.reshape(NZ, 8, size)
        total = jnp.concatenate([total[:, :, : size // 2], total[:, :, size // 2 :]], axis=1)
        Fz[:, :, half(h)] = total.astype(BF16)
        for i, off in enumerate(reach):
            src = Fz.at[turn(off), :, half(h)]
            go(remote(src, RZ.at[i, :, half(h)], zs.at[h, i], zr.at[h, i], place(x, turn(off), c, y)))

    def stage_f(h):
        lo, hi = halves(h)
        total = up(Fz[z, :, half(h)])
        for i in range(7):
            got(RZ.at[i, :, half(h)], zs.at[h, i], zr.at[h, i], dxp)
            total += up(RZ[i, :, half(h)])
        out_ref[:, lo] = total[:8].astype(BF16)
        out_ref[:, hi] = total[8:].astype(BF16)

    stages = [stage_a, stage_b, stage_c, stage_d, stage_e, stage_f]
    for i in range(nc + BACKWARD_LAGS[-1]):
        for n in BACKWARD_ORDER:
            lag, stage = BACKWARD_LAGS[n], stages[n]
            if 0 <= i - lag < nc:
                stage(i - lag)
    for i, (device, who) in enumerate(score):
        got(SB.at[who], ss.at[i], sr.at[i], device)
    dots = SB[0, :, 0, :] + SB[1, :, 0, :] + SB[2, :, 0, :] + SB[3, :, 0, :]
    fis_ref[0] = jnp.sum((sg[:, 1, :] * dots) ** 2) * (1.0 / 256.0)
    for copy in sent:
        copy.wait_send()


def backward(da, db, sg, un, wg, wu):
    width = wg.shape[0]
    chunks, start = [], 0
    for tiles in BACKWARD_TILES:
        chunks.append((start, tiles * 128))
        start += tiles * 128
    pieces = len(chunks)
    vm = pl.BlockSpec(memory_space=pltpu.VMEM)
    hbm = pl.BlockSpec(memory_space=pl.ANY)
    D = pltpu.SemaphoreType.DMA
    return pl.pallas_call(
        functools.partial(backward_kernel, chunks),
        out_shape=(jax.ShapeDtypeStruct((8, width), BF16), jax.ShapeDtypeStruct((1,), F32)),
        in_specs=[vm, vm, vm, vm, hbm, hbm],
        out_specs=(vm, pl.BlockSpec(memory_space=pltpu.SMEM)),
        scratch_shapes=[
            pltpu.VMEM((NY, 128, width), BF16),
            pltpu.VMEM((2, 128, width // 2), BF16),
            pltpu.VMEM((2, 128, width), BF16),
            pltpu.VMEM((NX, 64, width), BF16), pltpu.VMEM((NX, 64, width), BF16), pltpu.VMEM((NX, 64, width), BF16),
            pltpu.VMEM((3, 64, width), BF16),
            pltpu.VMEM((NZ, 16, width // 2), BF16),
            pltpu.VMEM((7, 16, width // 2), BF16),
            pltpu.VMEM((NY, NY, 8, META), F32),
            pltpu.VMEM((width, 256), BF16), pltpu.VMEM((width, 256), BF16),
            D((pieces, 2)), D((3,)), D((3,)), D((pieces, 4)), D((pieces, 4)), D((pieces,)), D((pieces,)),
            D((pieces, 3)), D((pieces, 3)), D((pieces, 7)), D((pieces, 7)),
        ],
        compiler_params=pltpu.CompilerParams(
            collective_id=2, has_side_effects=True, vmem_limit_bytes=60 << 20
        ),
        name="backward",
    )(da, db, sg, un, wg, wu)


def per_device(tokens, out_grads, expert_ids, gates, w_gate, w_up, w_down):
    group = lax.axis_index("dp")
    ids = lax.dynamic_slice_in_dim(expert_ids, group * 8, 8, 0).astype(BF16)
    own_gates = lax.dynamic_slice_in_dim(gates, group * 8, 8, 0)
    meta = jnp.pad(jnp.concatenate([ids, own_gates], axis=1), ((0, 0), (0, META - 16)))
    blk = jnp.concatenate(
        [jnp.concatenate([meta, meta], axis=0), jnp.concatenate([tokens, out_grads], axis=0)], axis=1
    )
    da, db, sg, un = forward(blk, w_gate[0], w_up[0], w_down[0])
    return backward(da, db, sg, un, w_gate[0], w_up[0])


def solution(mesh):
    placed = (
        P(("expert", "dp"), None), P(("expert", "dp"), None), P("expert", None), P("expert", None),
        P("expert", None, "dp"), P("expert", None, "dp"), P("expert", "dp", None),
    )
    return jax.shard_map(
        per_device, mesh=mesh, in_specs=placed,
        out_specs=(P(("expert", "dp"), None), P("expert")), check_vma=False,
    )
```

```python
import functools

import jax
import jax.numpy as jnp
from jax import lax
from jax.experimental import pallas as pl
from jax.experimental.pallas import tpu as pltpu
from jax.sharding import PartitionSpec as P

F32, BF16 = jnp.float32, jnp.bfloat16
NX, NZ, NC, NY = 4, 8, 2, 4
META = 128
LATE_TILES = (14, 18, 14)
EARLY_TILES = (10,)
LEAD, LAG = 0, 2
EARLY_SLOTS = (1, 2, 3, 4, 5, 9, 11, 12, 13, 14)
MUL = 3
BACKWARD_TILES = (8,) * 7
BACKWARD_LAGS = (0, 2, 3, 3, 4, 5)
BACKWARD_ORDER = (1, 2, 3, 4, 5, 0)
MESH = pl.DeviceIdType.MESH


def position():
    e = lax.axis_index("expert")
    return lax.div(e, NZ * NC), lax.rem(lax.div(e, NC), NZ), lax.rem(e, NC), lax.axis_index("dp")


def place(x, z, c, y):
    return {"expert": (x * NZ + z) * NC + c, "dp": y}


def remote(src, dst, send, recv, device):
    return pltpu.make_async_remote_copy(
        src_ref=src, dst_ref=dst, send_sem=send, recv_sem=recv, device_id=device, device_id_type=MESH
    )


def meet(peers):
    barrier = pltpu.get_barrier_semaphore()
    for peer in peers:
        pl.semaphore_signal(barrier, inc=1, device_id=peer, device_id_type=MESH)
    pl.semaphore_wait(barrier, len(peers))


def dot_nt(left, right):
    return lax.dot_general(left, right, (((1,), (1,)), ((), ())), preferred_element_type=F32)


def forward_kernel(
    chunks, early, blk, wg_hbm, wu_hbm, wd_hbm, da_ref, db_ref, sg_ref, un_ref,
    G, H, R, S, wg, wu, wd, acc, lsem, xs, xr, zs, zr, cs, cr, ys, yr,
    ks, kr, hys, hyr, hzs, hzr, hxs, hxr, hcs, hcr,
):
    x, z, c, y = position()
    e = lax.axis_index("expert")
    nc = len(chunks)
    xp, xm, xa = lax.rem(x + 1, NX), lax.rem(x + NX - 1, NX), lax.rem(x + 2, NX)
    zp, zm = lax.rem(z + 1, NZ), lax.rem(z + NZ - 1, NZ)
    yp, ym, ya = lax.rem(y + 1, NY), lax.rem(y + NY - 1, NY), lax.rem(y + 2, NY)
    co = 1 - c
    dxp, dxm = place(xp, z, c, y), place(xm, z, c, y)
    dzp, dzm = place(x, zp, c, y), place(x, zm, c, y)
    dyp, dym = place(x, z, c, yp), place(x, z, c, ym)
    dco = place(x, z, co, y)
    dya, dxa = place(x, z, c, ya), place(xa, z, c, y)
    wide = early[0][0]
    loads = [
        pltpu.make_async_copy(wg_hbm, wg, lsem.at[0]),
        pltpu.make_async_copy(wu_hbm, wu, lsem.at[1]),
        pltpu.make_async_copy(wd_hbm, wd, lsem.at[2]),
    ]
    for load in loads:
        load.start()
    G[z, x, c] = blk[:, :wide]
    H[x, c, z, y] = blk[:, wide:]
    meet([dxp, dxm, dxa, dzp, dzm, dyp, dym, dya, dco])
    sent = []

    def go(copy):
        copy.start()
        sent.append(copy)

    def cols(h):
        return pl.ds(chunks[h][0], chunks[h][1])

    def halves(h):
        start, size = chunks[h]
        first = size // 2 // 128 * 128
        return pl.ds(start, first), pl.ds(start + first, size - first)

    others_x = [(dxp, xm), (dxm, xp), (dxa, xa)]
    others_y = [(dyp, ym), (dym, yp), (dya, ya)]
    near = [0, -1, 1, -2, 2, -3, 3, 4]
    phases = [(0,), (1, 2), (3, 4), (5, 6), (7,)]

    def turn(off):
        return lax.rem(z + off + NZ, NZ)

    def ring(block, step, arriving):
        if step < 3:
            return [
                (block(-step - arriving, pl.ds(0, 4)), step, dzp),
                (block(step + arriving, pl.ds(0, 4)), 3 + step, dzm),
            ]
        return [
            (block(-step - arriving, pl.ds(0, 2)), 6, dzp),
            (block(step + arriving, pl.ds(2, 2)), 7, dzm),
        ]

    def ring_send(block, send, recv, step):
        for b, i, device in ring(block, step, 0):
            go(remote(b, b, send(i), recv(i), device))

    def ring_wait(block, send, recv, step):
        for b, i, device in ring(block, step, 1):
            remote(b, b, send(i), recv(i), device).wait_recv()

    def late_x(h):
        b = G.at[z, x, c, :, cols(h)]
        for i, (device, _) in enumerate(others_x):
            go(remote(b, b, xs.at[h, i], xr.at[h, i], device))

    def late_block(h):
        return lambda off, part: G.at[turn(off), part, c, :, cols(h)]

    def late_share(h, i):
        b = G.at[turn(near[i]), :, c, :, cols(h)]
        go(remote(b, b, cs.at[h, i], cr.at[h, i], dco))

    def late_near(h):
        for i, (device, who) in enumerate(others_x):
            b = G.at[z, who, c, :, cols(h)]
            remote(b, b, xs.at[h, i], xr.at[h, i], device).wait_recv()
        late_share(h, 0)

    def late_z(h):
        ring_send(late_block(h), lambda i: zs.at[h, i], lambda i: zr.at[h, i], 0)

    def late_advance(h, step):
        args = (late_block(h), lambda i: zs.at[h, i], lambda i: zr.at[h, i])
        ring_wait(*args, step)
        if step < 3:
            ring_send(*args, step + 1)
        for i in phases[step + 1]:
            late_share(h, i)

    rows = NX * NC * 16

    def routes(zz):
        meta = G[zz, :, :, :, 0:META].reshape(rows, META).astype(F32)
        lane = lax.broadcasted_iota(jnp.int32, (rows, META), 1)
        chosen = jnp.where(lane < 8, meta, -1.0) == e.astype(F32)
        gates = pltpu.roll(meta, META - 8, 1)
        hit = jnp.sum(chosen.astype(F32), axis=1, keepdims=True)
        gate = jnp.sum(jnp.where(chosen, gates, 0.0), axis=1, keepdims=True)
        r = lax.broadcasted_iota(jnp.int32, (rows, rows), 0)
        q = lax.broadcasted_iota(jnp.int32, (rows, rows), 1)
        earlier = jnp.where((r // 8 == q // 8) & (q < r), 1.0, 0.0).astype(BF16)
        hits = jnp.broadcast_to(hit, (rows, META))
        rank = jnp.dot(earlier, hits.astype(BF16), preferred_element_type=F32)
        slot = (r // 16 * 2).astype(F32) + rank
        lanes = lane.astype(F32)
        match = (lanes == slot + (r // 8 % 2 * 16).astype(F32)) & (hits > 0.5)
        S[y, zz] = jnp.transpose(jnp.where(match, 1.0, 0.0))[:32].astype(BF16)
        match = (lanes == slot + zz.astype(F32) * 16.0) & (hits > 0.5)
        give = jnp.where(match, jnp.broadcast_to(gate, (rows, META)), 0.0)
        un_ref[:, :, zz] = give.reshape(NX, NC, 16, META)[:, :, :8]

    def late_pack(h, i):
        zz = turn(near[i])
        b = G.at[zz, :, co, :, cols(h)]
        remote(b, b, cs.at[h, i], cr.at[h, i], dco).wait_recv()
        if h == 0:
            routes(zz)
        size = chunks[h][1]
        slab = G[zz, :, :, :, cols(h)].reshape(rows, size)
        got = jnp.dot(S[y, zz], slab, preferred_element_type=F32).astype(BF16)
        R[y, zz, :, :, cols(h)] = got.reshape(2, 16, size)
        b = R.at[y, zz, :, :, cols(h)]
        go(remote(b, b, ys.at[h, i, 0], yr.at[h, i, 0], dyp))
        go(remote(b, b, ys.at[h, i, 1], yr.at[h, i, 1], dym))

    def y_forward(h, i):
        zz = turn(near[i])
        lo, hi = halves(h)
        b = R.at[ym, zz, :, :, cols(h)]
        remote(b, b, ys.at[h, i, 0], yr.at[h, i, 0], dyp).wait_recv()
        b = R.at[ym, zz, :, :, lo]
        go(remote(b, b, ys.at[h, i, 2], yr.at[h, i, 2], dyp))
        b = R.at[yp, zz, :, :, cols(h)]
        remote(b, b, ys.at[h, i, 1], yr.at[h, i, 1], dym).wait_recv()
        b = R.at[yp, zz, :, :, hi]
        go(remote(b, b, ys.at[h, i, 3], yr.at[h, i, 3], dym))

    def y_last(h):
        lo, hi = halves(h)
        for i in range(NZ):
            zz = turn(near[i])
            b = R.at[ya, zz, :, :, lo]
            remote(b, b, ys.at[h, i, 2], yr.at[h, i, 2], dyp).wait_recv()
            b = R.at[ya, zz, :, :, hi]
            remote(b, b, ys.at[h, i, 3], yr.at[h, i, 3], dym).wait_recv()

    def multiply(start, size):
        if start == 0:
            start, size = META, size - META
            for load in loads:
                load.wait()
            acc[...] = jnp.zeros_like(acc)
        f = pl.ds(start - META, size)
        at = pl.ds(start, size)
        tok = R[:, :, 0, :, at].reshape(512, size)
        grad = R[:, :, 1, :, at].reshape(512, size)
        acc[0] += jnp.dot(tok, wg[f, :], preferred_element_type=F32)
        acc[1] += jnp.dot(tok, wu[f, :], preferred_element_type=F32)
        acc[2] += dot_nt(grad, wd[:, f])

    def own(q):
        return pl.ds(early[q][0] - wide, early[q][1])

    def early_y(q):
        b = H.at[x, c, z, y, :, own(q)]
        for i, (device, _) in enumerate(others_y):
            go(remote(b, b, hys.at[q, i], hyr.at[q, i], device))

    def early_block(q):
        return lambda off, part: H.at[x, c, turn(off), part, :, own(q)]

    def early_z(q):
        for i, (device, who) in enumerate(others_y):
            b = H.at[x, c, z, who, :, own(q)]
            remote(b, b, hys.at[q, i], hyr.at[q, i], device).wait_recv()
        ring_send(early_block(q), lambda i: hzs.at[q, i], lambda i: hzr.at[q, i], 0)

    def early_advance(q, step):
        args = (early_block(q), lambda i: hzs.at[q, i], lambda i: hzr.at[q, i])
        ring_wait(*args, step)
        if step < 3:
            ring_send(*args, step + 1)
        else:
            b = early_line(q, x, c)
            go(remote(b, b, hxs.at[q, 0], hxr.at[q, 0], dxp))
            go(remote(b, b, hxs.at[q, 1], hxr.at[q, 1], dxm))
            early_share(q, 0, x)

    def early_line(q, xx, cc, part=slice(None)):
        return H.at[xx, cc, part, :, :, own(q)]

    def early_share(q, i, xx):
        b = early_line(q, xx, c)
        go(remote(b, b, hcs.at[q, i], hcr.at[q, i], dco))

    def early_forward(q):
        for i, who, part, device in ((0, xm, pl.ds(0, 4), dxp), (1, xp, pl.ds(4, 4), dxm)):
            b = early_line(q, who, c)
            remote(b, b, hxs.at[q, i], hxr.at[q, i], device).wait_recv()
            b = early_line(q, who, c, part)
            go(remote(b, b, hxs.at[q, 2 + i], hxr.at[q, 2 + i], device))
            early_share(q, 1 + i, who)

    def early_last(q):
        for i, part, device in ((2, pl.ds(0, 4), dxp), (3, pl.ds(4, 4), dxm)):
            b = early_line(q, xa, c, part)
            remote(b, b, hxs.at[q, i], hxr.at[q, i], device).wait_recv()
        early_share(q, 3, xa)

    def early_arrived(q):
        for i, who in enumerate((x, xm, xp, xa)):
            b = early_line(q, who, co)
            remote(b, b, hcs.at[q, i], hcr.at[q, i], dco).wait_recv()

    def early_pack(q, some):
        if some == 0:
            early_arrived(q)
        start, size = early[q]

        def body(i, carry):
            g, zz = lax.div(i, NZ), lax.rem(i, NZ)
            slab = H[:, :, zz, g, :, own(q)].reshape(rows, size)
            got = jnp.dot(S[g, zz], slab, preferred_element_type=F32).astype(BF16)
            R[g, zz, :, :, pl.ds(start, size)] = got.reshape(2, 16, size)
            return carry

        lax.fori_loop(some * 16, some * 16 + 16, body, 0)

    def picks_arrived():
        for i, (device, who) in enumerate(others_y):
            remote(S.at[who], S.at[who], ks.at[i], kr.at[i], device).wait_recv()

    nq = len(early)
    todo = [[functools.partial(early_z, q) for q in range(nq)]]
    todo += [[functools.partial(early_advance, q, step) for q in range(nq)] for step in range(4)]
    todo += [[functools.partial(early_forward, q)] for q in range(nq)]
    todo += [[functools.partial(early_last, q)] for q in range(nq)]
    todo[-1].append(picks_arrived)
    todo += [[functools.partial(early_pack, q, some) for q in range(nq)] for some in (0, 1)]
    todo += [[functools.partial(multiply, *early[q]) for q in range(nq)]]
    slots = list(EARLY_SLOTS)

    late_x(0)
    for q in range(nq):
        early_y(q)
    for h in range(1, nc):
        late_x(h)
    while slots and slots[0] < 0:
        slots.pop(0)
        for event in todo.pop(0):
            event()
    late_near(0)
    late_z(0)
    for h in range(1, nc):
        late_near(h)
    ahead = []
    for h in range(nc):
        for step in range(-1, 4):
            ahead.append((max(0, 5 * h + step + 1 - (LEAD if h else 0)), h, step))
    ahead = [item for item in ahead if item[1:] != (0, -1)]
    ready = []

    def forward_until(slot):
        while ready and ready[0][0] <= slot:
            y_forward(*ready.pop(0)[1:])

    for slot in range(5 * nc):
        h, p = divmod(slot, 5)
        while ahead and ahead[0][0] <= slot:
            _, hh, step = ahead.pop(0)
            if step < 0:
                late_z(hh)
            else:
                late_advance(hh, step)
        now = [(hh, 0) for hh in range(nc)] if slot == 0 else [(h, i) for i in phases[p] if i]
        for item in now:
            late_pack(*item)
        forward_until(slot - LAG)
        ready += [(slot, *item) for item in now]
        if slot == 4:
            for i, (device, _) in enumerate(others_y):
                go(remote(S.at[y], S.at[y], ks.at[i], kr.at[i], device))
        while slots and slots[0] <= slot:
            slots.pop(0)
            for event in todo.pop(0):
                event()
        if h and p == MUL:
            forward_until(5 * h - 1)
            y_last(h - 1)
            multiply(*chunks[h - 1])
    forward_until(5 * nc)
    while todo:
        for event in todo.pop(0):
            event()
    y_last(nc - 1)
    multiply(*chunks[nc - 1])
    lane = lax.broadcasted_iota(jnp.int32, (128, META), 1)
    for g in range(4):
        at = pl.ds(g * 128, 128)
        a, b, u = acc[0, at, :], acc[1, at, :], acc[2, at, :]
        sig = jax.nn.sigmoid(a)
        active = a * sig
        s = jnp.sum(active * b * u, axis=1, keepdims=True)
        da_ref[at, :] = (u * b * sig * (1.0 + a * (1.0 - sig))).astype(BF16)
        db_ref[at, :] = (u * active).astype(BF16)
        meta = R[g, :, 0, :, 0:META].reshape(128, META).astype(F32)
        chosen = jnp.where(lane < 8, meta, -1.0) == e.astype(F32)
        gate = jnp.sum(jnp.where(chosen, pltpu.roll(meta, META - 8, 1), 0.0), axis=1, keepdims=True)
        sg_ref[g] = jnp.transpose(jnp.where(lane == 0, s, jnp.where(lane == 1, gate, 0.0)))[:8]
    for copy in sent:
        copy.wait_send()


def forward(blk, wg, wu, wd):
    width = blk.shape[1] - META
    chunks, start = [], 0
    for tiles in LATE_TILES + EARLY_TILES:
        size = tiles * 128 + (0 if start else META)
        chunks.append((start, size))
        start += size
    pieces, nq = len(LATE_TILES), len(EARLY_TILES)
    chunks, early = chunks[:pieces], chunks[pieces:]
    wide = early[0][0]
    vm = pl.BlockSpec(memory_space=pltpu.VMEM)
    hbm = pl.BlockSpec(memory_space=pl.ANY)
    D = pltpu.SemaphoreType.DMA
    shape = jax.ShapeDtypeStruct
    return pl.pallas_call(
        functools.partial(forward_kernel, chunks, early),
        out_shape=(
            shape((512, 256), BF16), shape((512, 256), BF16), shape((NY, 8, META), F32),
            shape((NX, NC, NZ, 8, META), F32),
        ),
        in_specs=[vm, hbm, hbm, hbm],
        out_specs=(vm, vm, vm, vm),
        scratch_shapes=[
            pltpu.VMEM((NZ, NX, NC, 16, wide), BF16),
            pltpu.VMEM((NX, NC, NZ, NY, 16, width + META - wide), BF16),
            pltpu.VMEM((NY, NZ, 2, 16, width + META), BF16),
            pltpu.VMEM((NY, NZ, 32, 128), BF16),
            pltpu.VMEM((width, 256), BF16), pltpu.VMEM((width, 256), BF16), pltpu.VMEM((256, width), BF16),
            pltpu.VMEM((3, 512, 256), F32),
            D((3,)), D((pieces, 3)), D((pieces, 3)), D((pieces, 8)), D((pieces, 8)),
            D((pieces, 8)), D((pieces, 8)), D((pieces, 8, 4)), D((pieces, 8, 4)),
            D((3,)), D((3,)), D((nq, 3)), D((nq, 3)), D((nq, 8)), D((nq, 8)),
            D((nq, 4)), D((nq, 4)), D((nq, 4)), D((nq, 4)),
        ],
        compiler_params=pltpu.CompilerParams(
            collective_id=1, has_side_effects=True, vmem_limit_bytes=60 << 20
        ),
        name="forward",
    )(blk, wg, wu, wd)


def backward_kernel(
    chunks, da, db, sg, un, wg_hbm, wu_hbm, out_ref, fis_ref,
    O, R1, R2, E, DS, RC, X, Fz, RZ, SB, wg, wu,
    lsem, ss, sr, ys, yr, cs, cr, xs, xr, zs, zr,
):
    x, z, c, y = position()
    nc = len(chunks)
    xp, xm, xa = lax.rem(x + 1, NX), lax.rem(x + NX - 1, NX), lax.rem(x + 2, NX)
    yp, ym, ya = lax.rem(y + 1, NY), lax.rem(y + NY - 1, NY), lax.rem(y + 2, NY)
    co = 1 - c
    dxp, dxm, dxa = place(xp, z, c, y), place(xm, z, c, y), place(xa, z, c, y)
    reach = (1, -1, 2, -2, 3, -3, 4)

    def turn(off):
        return lax.rem(z + off + NZ, NZ)

    dyp, dym, dya = place(x, z, c, yp), place(x, z, c, ym), place(x, z, c, ya)
    dco = place(x, z, co, y)

    def rows_of(h):
        return pl.ds(chunks[h][0], chunks[h][1])

    loads = []
    for h in range(nc):
        for i, (src, dst) in enumerate(((wg_hbm, wg), (wu_hbm, wu))):
            load = pltpu.make_async_copy(src.at[rows_of(h), :], dst.at[rows_of(h), :], lsem.at[h, i])
            load.start()
            loads.append(load)
    SB[y] = sg[...]
    meet([dxp, dxm, dxa, dyp, dym, dya, dco] + [place(x, turn(off), c, y) for off in reach])
    sent = []

    def go(copy):
        copy.start()
        sent.append(copy)

    def got(dst, send, recv, device):
        remote(dst, dst, send, recv, device).wait_recv()

    score = [(dyp, ym), (dym, yp), (dya, ya)]
    for i, (device, _) in enumerate(score):
        go(remote(SB.at[y], SB.at[y], ss.at[i], sr.at[i], device))

    def halves(h):
        start, size = chunks[h]
        return pl.ds(start, size // 2), pl.ds(start + size // 2, size // 2)

    def half(h):
        start, size = chunks[h]
        return pl.ds(start // 2, size // 2)

    def up(v):
        return v.astype(F32)

    def stage_a(h):
        at = rows_of(h)
        loads[2 * h].wait()
        loads[2 * h + 1].wait()
        part = dot_nt(da[...], wg[at, :]) + dot_nt(db[...], wu[at, :])
        O[:, :, at] = part.astype(BF16).reshape(NY, 128, chunks[h][1])
        lo, hi = halves(h)
        go(remote(O.at[ya, :, lo], R1.at[0, :, half(h)], ys.at[h, 0], yr.at[h, 0], dyp))
        go(remote(O.at[ya, :, hi], R1.at[1, :, half(h)], ys.at[h, 1], yr.at[h, 1], dym))

    def stage_b(h):
        at = rows_of(h)
        lo, hi = halves(h)
        got(R1.at[0, :, half(h)], ys.at[h, 0], yr.at[h, 0], dyp)
        O[yp, :, lo] = (up(O[yp, :, lo]) + up(R1[0, :, half(h)])).astype(BF16)
        go(remote(O.at[yp, :, at], R2.at[0, :, at], ys.at[h, 2], yr.at[h, 2], dyp))
        got(R1.at[1, :, half(h)], ys.at[h, 1], yr.at[h, 1], dym)
        O[ym, :, hi] = (up(O[ym, :, hi]) + up(R1[1, :, half(h)])).astype(BF16)
        go(remote(O.at[ym, :, at], R2.at[1, :, at], ys.at[h, 3], yr.at[h, 3], dym))

    def stage_c(h):
        at = rows_of(h)
        got(R2.at[0, :, at], ys.at[h, 2], yr.at[h, 2], dyp)
        got(R2.at[1, :, at], ys.at[h, 3], yr.at[h, 3], dym)
        back = (up(O[y, :, at]) + up(R2[0, :, at]) + up(R2[1, :, at])).astype(BF16)
        for t in range(NX):
            mine = un[t, c].reshape(64, META).astype(BF16)
            theirs = un[t, co].reshape(64, META).astype(BF16)
            DS[t, :, at] = jnp.dot(theirs, back, preferred_element_type=F32).astype(BF16)
            E[t, :, at] = jnp.dot(mine, back, preferred_element_type=F32).astype(BF16)
        go(remote(DS.at[:, :, at], RC.at[:, :, at], cs.at[h], cr.at[h], dco))

    def stage_d(h):
        at = rows_of(h)
        got(RC.at[:, :, at], cs.at[h], cr.at[h], dco)
        E[:, :, at] = (up(E[:, :, at]) + up(RC[:, :, at])).astype(BF16)
        for i, (who, device) in enumerate(((xp, dxp), (xm, dxm), (xa, dxa))):
            go(remote(E.at[who, :, at], X.at[i, :, at], xs.at[h, i], xr.at[h, i], device))

    def stage_e(h):
        at = rows_of(h)
        total = up(E[x, :, at])
        for i in range(3):
            got(X.at[i, :, at], xs.at[h, i], xr.at[h, i], dxp)
            total += up(X[i, :, at])
        size = chunks[h][1]
        total = total.reshape(NZ, 8, size)
        total = jnp.concatenate([total[:, :, : size // 2], total[:, :, size // 2 :]], axis=1)
        Fz[:, :, half(h)] = total.astype(BF16)
        for i, off in enumerate(reach):
            src = Fz.at[turn(off), :, half(h)]
            go(remote(src, RZ.at[i, :, half(h)], zs.at[h, i], zr.at[h, i], place(x, turn(off), c, y)))

    def stage_f(h):
        lo, hi = halves(h)
        total = up(Fz[z, :, half(h)])
        for i in range(7):
            got(RZ.at[i, :, half(h)], zs.at[h, i], zr.at[h, i], dxp)
            total += up(RZ[i, :, half(h)])
        out_ref[:, lo] = total[:8].astype(BF16)
        out_ref[:, hi] = total[8:].astype(BF16)

    stages = [stage_a, stage_b, stage_c, stage_d, stage_e, stage_f]
    for i in range(nc + BACKWARD_LAGS[-1]):
        for n in BACKWARD_ORDER:
            lag, stage = BACKWARD_LAGS[n], stages[n]
            if 0 <= i - lag < nc:
                stage(i - lag)
    for i, (device, who) in enumerate(score):
        got(SB.at[who], ss.at[i], sr.at[i], device)
    dots = SB[0, :, 0, :] + SB[1, :, 0, :] + SB[2, :, 0, :] + SB[3, :, 0, :]
    fis_ref[0] = jnp.sum((sg[:, 1, :] * dots) ** 2) * (1.0 / 256.0)
    for copy in sent:
        copy.wait_send()


def backward(da, db, sg, un, wg, wu):
    width = wg.shape[0]
    chunks, start = [], 0
    for tiles in BACKWARD_TILES:
        chunks.append((start, tiles * 128))
        start += tiles * 128
    pieces = len(chunks)
    vm = pl.BlockSpec(memory_space=pltpu.VMEM)
    hbm = pl.BlockSpec(memory_space=pl.ANY)
    D = pltpu.SemaphoreType.DMA
    return pl.pallas_call(
        functools.partial(backward_kernel, chunks),
        out_shape=(jax.ShapeDtypeStruct((8, width), BF16), jax.ShapeDtypeStruct((1,), F32)),
        in_specs=[vm, vm, vm, vm, hbm, hbm],
        out_specs=(vm, pl.BlockSpec(memory_space=pltpu.SMEM)),
        scratch_shapes=[
            pltpu.VMEM((NY, 128, width), BF16),
            pltpu.VMEM((2, 128, width // 2), BF16),
            pltpu.VMEM((2, 128, width), BF16),
            pltpu.VMEM((NX, 64, width), BF16), pltpu.VMEM((NX, 64, width), BF16), pltpu.VMEM((NX, 64, width), BF16),
            pltpu.VMEM((3, 64, width), BF16),
            pltpu.VMEM((NZ, 16, width // 2), BF16),
            pltpu.VMEM((7, 16, width // 2), BF16),
            pltpu.VMEM((NY, NY, 8, META), F32),
            pltpu.VMEM((width, 256), BF16), pltpu.VMEM((width, 256), BF16),
            D((pieces, 2)), D((3,)), D((3,)), D((pieces, 4)), D((pieces, 4)), D((pieces,)), D((pieces,)),
            D((pieces, 3)), D((pieces, 3)), D((pieces, 7)), D((pieces, 7)),
        ],
        compiler_params=pltpu.CompilerParams(
            collective_id=2, has_side_effects=True, vmem_limit_bytes=60 << 20
        ),
        name="backward",
    )(da, db, sg, un, wg, wu)


def per_device(tokens, out_grads, expert_ids, gates, w_gate, w_up, w_down):
    group = lax.axis_index("dp")
    ids = lax.dynamic_slice_in_dim(expert_ids, group * 8, 8, 0).astype(BF16)
    own_gates = lax.dynamic_slice_in_dim(gates, group * 8, 8, 0)
    meta = jnp.pad(jnp.concatenate([ids, own_gates], axis=1), ((0, 0), (0, META - 16)))
    blk = jnp.concatenate(
        [jnp.concatenate([meta, meta], axis=0), jnp.concatenate([tokens, out_grads], axis=0)], axis=1
    )
    da, db, sg, un = forward(blk, w_gate[0], w_up[0], w_down[0])
    return backward(da, db, sg, un, w_gate[0], w_up[0])


def solution(mesh):
    placed = (
        P(("expert", "dp"), None), P(("expert", "dp"), None), P("expert", None), P("expert", None),
        P("expert", None, "dp"), P("expert", None, "dp"), P("expert", "dp", None),
    )
    return jax.shard_map(
        per_device, mesh=mesh, in_specs=placed,
        out_specs=(P(("expert", "dp"), None), P("expert")), check_vma=False,
    )
```

```python
import functools

import jax
import jax.numpy as jnp
from jax import lax
from jax.experimental import pallas as pl
from jax.experimental.pallas import tpu as pltpu
from jax.sharding import PartitionSpec as P

F32, BF16 = jnp.float32, jnp.bfloat16
NX, NZ, NC, NY = 4, 8, 2, 4
META = 128
LATE_TILES = (14, 18, 14)
EARLY_TILES = (10,)
LEAD, LAG = 0, 2
EARLY_SLOTS = (1, 2, 3, 4, 5, 9, 12, 13, 14, 99)
MUL = 3
BACKWARD_TILES = (8,) * 7
BACKWARD_LAGS = (0, 2, 3, 3, 4, 5)
BACKWARD_ORDER = (1, 2, 3, 4, 5, 0)
MESH = pl.DeviceIdType.MESH


def position():
    e = lax.axis_index("expert")
    return lax.div(e, NZ * NC), lax.rem(lax.div(e, NC), NZ), lax.rem(e, NC), lax.axis_index("dp")


def place(x, z, c, y):
    return {"expert": (x * NZ + z) * NC + c, "dp": y}


def remote(src, dst, send, recv, device):
    return pltpu.make_async_remote_copy(
        src_ref=src, dst_ref=dst, send_sem=send, recv_sem=recv, device_id=device, device_id_type=MESH
    )


def meet(peers):
    barrier = pltpu.get_barrier_semaphore()
    for peer in peers:
        pl.semaphore_signal(barrier, inc=1, device_id=peer, device_id_type=MESH)
    pl.semaphore_wait(barrier, len(peers))


def dot_nt(left, right):
    return lax.dot_general(left, right, (((1,), (1,)), ((), ())), preferred_element_type=F32)


def forward_kernel(
    chunks, early, blk, wg_hbm, wu_hbm, wd_hbm, da_ref, db_ref, sg_ref, un_ref,
    G, H, R, S, wg, wu, wd, acc, lsem, xs, xr, zs, zr, cs, cr, ys, yr,
    ks, kr, hys, hyr, hzs, hzr, hxs, hxr, hcs, hcr,
):
    x, z, c, y = position()
    e = lax.axis_index("expert")
    nc = len(chunks)
    xp, xm, xa = lax.rem(x + 1, NX), lax.rem(x + NX - 1, NX), lax.rem(x + 2, NX)
    zp, zm = lax.rem(z + 1, NZ), lax.rem(z + NZ - 1, NZ)
    yp, ym, ya = lax.rem(y + 1, NY), lax.rem(y + NY - 1, NY), lax.rem(y + 2, NY)
    co = 1 - c
    dxp, dxm = place(xp, z, c, y), place(xm, z, c, y)
    dzp, dzm = place(x, zp, c, y), place(x, zm, c, y)
    dyp, dym = place(x, z, c, yp), place(x, z, c, ym)
    dco = place(x, z, co, y)
    dya, dxa = place(x, z, c, ya), place(xa, z, c, y)
    wide = early[0][0]
    loads = [
        pltpu.make_async_copy(wg_hbm, wg, lsem.at[0]),
        pltpu.make_async_copy(wu_hbm, wu, lsem.at[1]),
        pltpu.make_async_copy(wd_hbm, wd, lsem.at[2]),
    ]
    for load in loads:
        load.start()
    G[z, x, c] = blk[:, :wide]
    H[x, c, z, y] = blk[:, wide:]
    meet([dxp, dxm, dxa, dzp, dzm, dyp, dym, dya, dco])
    sent = []

    def go(copy):
        copy.start()
        sent.append(copy)

    def cols(h):
        return pl.ds(chunks[h][0], chunks[h][1])

    def halves(h):
        start, size = chunks[h]
        first = size // 2 // 128 * 128
        return pl.ds(start, first), pl.ds(start + first, size - first)

    others_x = [(dxp, xm), (dxm, xp), (dxa, xa)]
    others_y = [(dyp, ym), (dym, yp), (dya, ya)]
    near = [0, -1, 1, -2, 2, -3, 3, 4]
    phases = [(0,), (1, 2), (3, 4), (5, 6), (7,)]

    def turn(off):
        return lax.rem(z + off + NZ, NZ)

    def ring(block, step, arriving):
        if step < 3:
            return [
                (block(-step - arriving, pl.ds(0, 4)), step, dzp),
                (block(step + arriving, pl.ds(0, 4)), 3 + step, dzm),
            ]
        return [
            (block(-step - arriving, pl.ds(0, 2)), 6, dzp),
            (block(step + arriving, pl.ds(2, 2)), 7, dzm),
        ]

    def ring_send(block, send, recv, step):
        for b, i, device in ring(block, step, 0):
            go(remote(b, b, send(i), recv(i), device))

    def ring_wait(block, send, recv, step):
        for b, i, device in ring(block, step, 1):
            remote(b, b, send(i), recv(i), device).wait_recv()

    def late_x(h):
        b = G.at[z, x, c, :, cols(h)]
        for i, (device, _) in enumerate(others_x):
            go(remote(b, b, xs.at[h, i], xr.at[h, i], device))

    def late_block(h):
        return lambda off, part: G.at[turn(off), part, c, :, cols(h)]

    def late_share(h, i):
        b = G.at[turn(near[i]), :, c, :, cols(h)]
        go(remote(b, b, cs.at[h, i], cr.at[h, i], dco))

    def late_near(h):
        for i, (device, who) in enumerate(others_x):
            b = G.at[z, who, c, :, cols(h)]
            remote(b, b, xs.at[h, i], xr.at[h, i], device).wait_recv()
        late_share(h, 0)

    def late_z(h):
        ring_send(late_block(h), lambda i: zs.at[h, i], lambda i: zr.at[h, i], 0)

    def late_advance(h, step):
        args = (late_block(h), lambda i: zs.at[h, i], lambda i: zr.at[h, i])
        ring_wait(*args, step)
        if step < 3:
            ring_send(*args, step + 1)
        for i in phases[step + 1]:
            late_share(h, i)

    rows = NX * NC * 16

    def routes(zz):
        meta = G[zz, :, :, :, 0:META].reshape(rows, META).astype(F32)
        lane = lax.broadcasted_iota(jnp.int32, (rows, META), 1)
        chosen = jnp.where(lane < 8, meta, -1.0) == e.astype(F32)
        gates = pltpu.roll(meta, META - 8, 1)
        hit = jnp.sum(chosen.astype(F32), axis=1, keepdims=True)
        gate = jnp.sum(jnp.where(chosen, gates, 0.0), axis=1, keepdims=True)
        r = lax.broadcasted_iota(jnp.int32, (rows, rows), 0)
        q = lax.broadcasted_iota(jnp.int32, (rows, rows), 1)
        earlier = jnp.where((r // 8 == q // 8) & (q < r), 1.0, 0.0).astype(BF16)
        hits = jnp.broadcast_to(hit, (rows, META))
        rank = jnp.dot(earlier, hits.astype(BF16), preferred_element_type=F32)
        slot = (r // 16 * 2).astype(F32) + rank
        lanes = lane.astype(F32)
        match = (lanes == slot + (r // 8 % 2 * 16).astype(F32)) & (hits > 0.5)
        S[y, zz] = jnp.transpose(jnp.where(match, 1.0, 0.0))[:32].astype(BF16)
        match = (lanes == slot + zz.astype(F32) * 16.0) & (hits > 0.5)
        give = jnp.where(match, jnp.broadcast_to(gate, (rows, META)), 0.0)
        un_ref[:, :, zz] = give.reshape(NX, NC, 16, META)[:, :, :8]

    def late_pack(h, i):
        zz = turn(near[i])
        b = G.at[zz, :, co, :, cols(h)]
        remote(b, b, cs.at[h, i], cr.at[h, i], dco).wait_recv()
        if h == 0:
            routes(zz)
        size = chunks[h][1]
        slab = G[zz, :, :, :, cols(h)].reshape(rows, size)
        got = jnp.dot(S[y, zz], slab, preferred_element_type=F32).astype(BF16)
        R[y, zz, :, :, cols(h)] = got.reshape(2, 16, size)
        b = R.at[y, zz, :, :, cols(h)]
        go(remote(b, b, ys.at[h, i, 0], yr.at[h, i, 0], dyp))
        go(remote(b, b, ys.at[h, i, 1], yr.at[h, i, 1], dym))

    def y_forward(h, i):
        zz = turn(near[i])
        lo, hi = halves(h)
        b = R.at[ym, zz, :, :, cols(h)]
        remote(b, b, ys.at[h, i, 0], yr.at[h, i, 0], dyp).wait_recv()
        b = R.at[ym, zz, :, :, lo]
        go(remote(b, b, ys.at[h, i, 2], yr.at[h, i, 2], dyp))
        b = R.at[yp, zz, :, :, cols(h)]
        remote(b, b, ys.at[h, i, 1], yr.at[h, i, 1], dym).wait_recv()
        b = R.at[yp, zz, :, :, hi]
        go(remote(b, b, ys.at[h, i, 3], yr.at[h, i, 3], dym))

    def y_last(h):
        lo, hi = halves(h)
        for i in range(NZ):
            zz = turn(near[i])
            b = R.at[ya, zz, :, :, lo]
            remote(b, b, ys.at[h, i, 2], yr.at[h, i, 2], dyp).wait_recv()
            b = R.at[ya, zz, :, :, hi]
            remote(b, b, ys.at[h, i, 3], yr.at[h, i, 3], dym).wait_recv()

    def multiply(start, size):
        if start == 0:
            start, size = META, size - META
            for load in loads:
                load.wait()
            acc[...] = jnp.zeros_like(acc)
        f = pl.ds(start - META, size)
        at = pl.ds(start, size)
        tok = R[:, :, 0, :, at].reshape(512, size)
        grad = R[:, :, 1, :, at].reshape(512, size)
        acc[0] += jnp.dot(tok, wg[f, :], preferred_element_type=F32)
        acc[1] += jnp.dot(tok, wu[f, :], preferred_element_type=F32)
        acc[2] += dot_nt(grad, wd[:, f])

    def own(q):
        return pl.ds(early[q][0] - wide, early[q][1])

    def early_y(q):
        b = H.at[x, c, z, y, :, own(q)]
        for i, (device, _) in enumerate(others_y):
            go(remote(b, b, hys.at[q, i], hyr.at[q, i], device))

    def early_block(q):
        return lambda off, part: H.at[x, c, turn(off), part, :, own(q)]

    def early_z(q):
        for i, (device, who) in enumerate(others_y):
            b = H.at[x, c, z, who, :, own(q)]
            remote(b, b, hys.at[q, i], hyr.at[q, i], device).wait_recv()
        ring_send(early_block(q), lambda i: hzs.at[q, i], lambda i: hzr.at[q, i], 0)

    def early_advance(q, step):
        args = (early_block(q), lambda i: hzs.at[q, i], lambda i: hzr.at[q, i])
        ring_wait(*args, step)
        if step < 3:
            ring_send(*args, step + 1)
        else:
            b = early_line(q, x, c)
            go(remote(b, b, hxs.at[q, 0], hxr.at[q, 0], dxp))
            go(remote(b, b, hxs.at[q, 1], hxr.at[q, 1], dxm))
            early_share(q, 0, x)

    def early_line(q, xx, cc, part=slice(None)):
        return H.at[xx, cc, part, :, :, own(q)]

    def early_share(q, i, xx):
        b = early_line(q, xx, c)
        go(remote(b, b, hcs.at[q, i], hcr.at[q, i], dco))

    def early_forward(q):
        for i, who, part, device in ((0, xm, pl.ds(0, 4), dxp), (1, xp, pl.ds(4, 4), dxm)):
            b = early_line(q, who, c)
            remote(b, b, hxs.at[q, i], hxr.at[q, i], device).wait_recv()
            b = early_line(q, who, c, part)
            go(remote(b, b, hxs.at[q, 2 + i], hxr.at[q, 2 + i], device))
            early_share(q, 1 + i, who)

    def early_last(q):
        for i, part, device in ((2, pl.ds(0, 4), dxp), (3, pl.ds(4, 4), dxm)):
            b = early_line(q, xa, c, part)
            remote(b, b, hxs.at[q, i], hxr.at[q, i], device).wait_recv()
        early_share(q, 3, xa)

    def early_arrived(q):
        for i, who in enumerate((x, xm, xp, xa)):
            b = early_line(q, who, co)
            remote(b, b, hcs.at[q, i], hcr.at[q, i], dco).wait_recv()

    def early_pack(q, some):
        if some == 0:
            early_arrived(q)
        start, size = early[q]

        def body(i, carry):
            g, zz = lax.div(i, NZ), lax.rem(i, NZ)
            slab = H[:, :, zz, g, :, own(q)].reshape(rows, size)
            got = jnp.dot(S[g, zz], slab, preferred_element_type=F32).astype(BF16)
            R[g, zz, :, :, pl.ds(start, size)] = got.reshape(2, 16, size)
            return carry

        lax.fori_loop(some * 16, some * 16 + 16, body, 0)

    def picks_arrived():
        for i, (device, who) in enumerate(others_y):
            remote(S.at[who], S.at[who], ks.at[i], kr.at[i], device).wait_recv()

    nq = len(early)
    todo = [[functools.partial(early_z, q) for q in range(nq)]]
    todo += [[functools.partial(early_advance, q, step) for q in range(nq)] for step in range(4)]
    todo += [[functools.partial(early_forward, q)] for q in range(nq)]
    todo += [[functools.partial(early_last, q)] for q in range(nq)]
    todo[-1].append(picks_arrived)
    todo += [[functools.partial(early_pack, q, some) for q in range(nq)] for some in (0, 1)]
    todo += [[functools.partial(multiply, *early[q]) for q in range(nq)]]
    slots = list(EARLY_SLOTS)

    late_x(0)
    for q in range(nq):
        early_y(q)
    for h in range(1, nc):
        late_x(h)
    while slots and slots[0] < 0:
        slots.pop(0)
        for event in todo.pop(0):
            event()
    late_near(0)
    late_z(0)
    for h in range(1, nc):
        late_near(h)
    ahead = []
    for h in range(nc):
        for step in range(-1, 4):
            ahead.append((max(0, 5 * h + step + 1 - (LEAD if h else 0)), h, step))
    ahead = [item for item in ahead if item[1:] != (0, -1)]
    ready = []

    def forward_until(slot):
        while ready and ready[0][0] <= slot:
            y_forward(*ready.pop(0)[1:])

    for slot in range(5 * nc):
        h, p = divmod(slot, 5)
        while ahead and ahead[0][0] <= slot:
            _, hh, step = ahead.pop(0)
            if step < 0:
                late_z(hh)
            else:
                late_advance(hh, step)
        now = [(hh, 0) for hh in range(nc)] if slot == 0 else [(h, i) for i in phases[p] if i]
        for item in now:
            late_pack(*item)
        forward_until(slot - LAG)
        ready += [(slot, *item) for item in now]
        if slot == 4:
            for i, (device, _) in enumerate(others_y):
                go(remote(S.at[y], S.at[y], ks.at[i], kr.at[i], device))
        while slots and slots[0] <= slot:
            slots.pop(0)
            for event in todo.pop(0):
                event()
        if h and p == MUL:
            forward_until(5 * h - 1)
            y_last(h - 1)
            multiply(*chunks[h - 1])
    forward_until(5 * nc)
    while todo:
        for event in todo.pop(0):
            event()
    y_last(nc - 1)
    multiply(*chunks[nc - 1])
    lane = lax.broadcasted_iota(jnp.int32, (128, META), 1)
    for g in range(4):
        at = pl.ds(g * 128, 128)
        a, b, u = acc[0, at, :], acc[1, at, :], acc[2, at, :]
        sig = jax.nn.sigmoid(a)
        active = a * sig
        s = jnp.sum(active * b * u, axis=1, keepdims=True)
        da_ref[at, :] = (u * b * sig * (1.0 + a * (1.0 - sig))).astype(BF16)
        db_ref[at, :] = (u * active).astype(BF16)
        meta = R[g, :, 0, :, 0:META].reshape(128, META).astype(F32)
        chosen = jnp.where(lane < 8, meta, -1.0) == e.astype(F32)
        gate = jnp.sum(jnp.where(chosen, pltpu.roll(meta, META - 8, 1), 0.0), axis=1, keepdims=True)
        sg_ref[g] = jnp.transpose(jnp.where(lane == 0, s, jnp.where(lane == 1, gate, 0.0)))[:8]
    for copy in sent:
        copy.wait_send()


def forward(blk, wg, wu, wd):
    width = blk.shape[1] - META
    chunks, start = [], 0
    for tiles in LATE_TILES + EARLY_TILES:
        size = tiles * 128 + (0 if start else META)
        chunks.append((start, size))
        start += size
    pieces, nq = len(LATE_TILES), len(EARLY_TILES)
    chunks, early = chunks[:pieces], chunks[pieces:]
    wide = early[0][0]
    vm = pl.BlockSpec(memory_space=pltpu.VMEM)
    hbm = pl.BlockSpec(memory_space=pl.ANY)
    D = pltpu.SemaphoreType.DMA
    shape = jax.ShapeDtypeStruct
    return pl.pallas_call(
        functools.partial(forward_kernel, chunks, early),
        out_shape=(
            shape((512, 256), BF16), shape((512, 256), BF16), shape((NY, 8, META), F32),
            shape((NX, NC, NZ, 8, META), F32),
        ),
        in_specs=[vm, hbm, hbm, hbm],
        out_specs=(vm, vm, vm, vm),
        scratch_shapes=[
            pltpu.VMEM((NZ, NX, NC, 16, wide), BF16),
            pltpu.VMEM((NX, NC, NZ, NY, 16, width + META - wide), BF16),
            pltpu.VMEM((NY, NZ, 2, 16, width + META), BF16),
            pltpu.VMEM((NY, NZ, 32, 128), BF16),
            pltpu.VMEM((width, 256), BF16), pltpu.VMEM((width, 256), BF16), pltpu.VMEM((256, width), BF16),
            pltpu.VMEM((3, 512, 256), F32),
            D((3,)), D((pieces, 3)), D((pieces, 3)), D((pieces, 8)), D((pieces, 8)),
            D((pieces, 8)), D((pieces, 8)), D((pieces, 8, 4)), D((pieces, 8, 4)),
            D((3,)), D((3,)), D((nq, 3)), D((nq, 3)), D((nq, 8)), D((nq, 8)),
            D((nq, 4)), D((nq, 4)), D((nq, 4)), D((nq, 4)),
        ],
        compiler_params=pltpu.CompilerParams(
            collective_id=1, has_side_effects=True, vmem_limit_bytes=60 << 20
        ),
        name="forward",
    )(blk, wg, wu, wd)


def backward_kernel(
    chunks, da, db, sg, un, wg_hbm, wu_hbm, out_ref, fis_ref,
    O, R1, R2, E, DS, RC, X, Fz, RZ, SB, wg, wu,
    lsem, ss, sr, ys, yr, cs, cr, xs, xr, zs, zr,
):
    x, z, c, y = position()
    nc = len(chunks)
    xp, xm, xa = lax.rem(x + 1, NX), lax.rem(x + NX - 1, NX), lax.rem(x + 2, NX)
    yp, ym, ya = lax.rem(y + 1, NY), lax.rem(y + NY - 1, NY), lax.rem(y + 2, NY)
    co = 1 - c
    dxp, dxm, dxa = place(xp, z, c, y), place(xm, z, c, y), place(xa, z, c, y)
    reach = (1, -1, 2, -2, 3, -3, 4)

    def turn(off):
        return lax.rem(z + off + NZ, NZ)

    dyp, dym, dya = place(x, z, c, yp), place(x, z, c, ym), place(x, z, c, ya)
    dco = place(x, z, co, y)

    def rows_of(h):
        return pl.ds(chunks[h][0], chunks[h][1])

    loads = []
    for h in range(nc):
        for i, (src, dst) in enumerate(((wg_hbm, wg), (wu_hbm, wu))):
            load = pltpu.make_async_copy(src.at[rows_of(h), :], dst.at[rows_of(h), :], lsem.at[h, i])
            load.start()
            loads.append(load)
    SB[y] = sg[...]
    meet([dxp, dxm, dxa, dyp, dym, dya, dco] + [place(x, turn(off), c, y) for off in reach])
    sent = []

    def go(copy):
        copy.start()
        sent.append(copy)

    def got(dst, send, recv, device):
        remote(dst, dst, send, recv, device).wait_recv()

    score = [(dyp, ym), (dym, yp), (dya, ya)]
    for i, (device, _) in enumerate(score):
        go(remote(SB.at[y], SB.at[y], ss.at[i], sr.at[i], device))

    def halves(h):
        start, size = chunks[h]
        return pl.ds(start, size // 2), pl.ds(start + size // 2, size // 2)

    def half(h):
        start, size = chunks[h]
        return pl.ds(start // 2, size // 2)

    def up(v):
        return v.astype(F32)

    def stage_a(h):
        at = rows_of(h)
        loads[2 * h].wait()
        loads[2 * h + 1].wait()
        part = dot_nt(da[...], wg[at, :]) + dot_nt(db[...], wu[at, :])
        O[:, :, at] = part.astype(BF16).reshape(NY, 128, chunks[h][1])
        lo, hi = halves(h)
        go(remote(O.at[ya, :, lo], R1.at[0, :, half(h)], ys.at[h, 0], yr.at[h, 0], dyp))
        go(remote(O.at[ya, :, hi], R1.at[1, :, half(h)], ys.at[h, 1], yr.at[h, 1], dym))

    def stage_b(h):
        at = rows_of(h)
        lo, hi = halves(h)
        got(R1.at[0, :, half(h)], ys.at[h, 0], yr.at[h, 0], dyp)
        O[yp, :, lo] = (up(O[yp, :, lo]) + up(R1[0, :, half(h)])).astype(BF16)
        go(remote(O.at[yp, :, at], R2.at[0, :, at], ys.at[h, 2], yr.at[h, 2], dyp))
        got(R1.at[1, :, half(h)], ys.at[h, 1], yr.at[h, 1], dym)
        O[ym, :, hi] = (up(O[ym, :, hi]) + up(R1[1, :, half(h)])).astype(BF16)
        go(remote(O.at[ym, :, at], R2.at[1, :, at], ys.at[h, 3], yr.at[h, 3], dym))

    def stage_c(h):
        at = rows_of(h)
        got(R2.at[0, :, at], ys.at[h, 2], yr.at[h, 2], dyp)
        got(R2.at[1, :, at], ys.at[h, 3], yr.at[h, 3], dym)
        back = (up(O[y, :, at]) + up(R2[0, :, at]) + up(R2[1, :, at])).astype(BF16)
        for t in range(NX):
            mine = un[t, c].reshape(64, META).astype(BF16)
            theirs = un[t, co].reshape(64, META).astype(BF16)
            DS[t, :, at] = jnp.dot(theirs, back, preferred_element_type=F32).astype(BF16)
            E[t, :, at] = jnp.dot(mine, back, preferred_element_type=F32).astype(BF16)
        go(remote(DS.at[:, :, at], RC.at[:, :, at], cs.at[h], cr.at[h], dco))

    def stage_d(h):
        at = rows_of(h)
        got(RC.at[:, :, at], cs.at[h], cr.at[h], dco)
        E[:, :, at] = (up(E[:, :, at]) + up(RC[:, :, at])).astype(BF16)
        for i, (who, device) in enumerate(((xp, dxp), (xm, dxm), (xa, dxa))):
            go(remote(E.at[who, :, at], X.at[i, :, at], xs.at[h, i], xr.at[h, i], device))

    def stage_e(h):
        at = rows_of(h)
        total = up(E[x, :, at])
        for i in range(3):
            got(X.at[i, :, at], xs.at[h, i], xr.at[h, i], dxp)
            total += up(X[i, :, at])
        size = chunks[h][1]
        total = total.reshape(NZ, 8, size)
        total = jnp.concatenate([total[:, :, : size // 2], total[:, :, size // 2 :]], axis=1)
        Fz[:, :, half(h)] = total.astype(BF16)
        for i, off in enumerate(reach):
            src = Fz.at[turn(off), :, half(h)]
            go(remote(src, RZ.at[i, :, half(h)], zs.at[h, i], zr.at[h, i], place(x, turn(off), c, y)))

    def stage_f(h):
        lo, hi = halves(h)
        total = up(Fz[z, :, half(h)])
        for i in range(7):
            got(RZ.at[i, :, half(h)], zs.at[h, i], zr.at[h, i], dxp)
            total += up(RZ[i, :, half(h)])
        out_ref[:, lo] = total[:8].astype(BF16)
        out_ref[:, hi] = total[8:].astype(BF16)

    stages = [stage_a, stage_b, stage_c, stage_d, stage_e, stage_f]
    for i in range(nc + BACKWARD_LAGS[-1]):
        for n in BACKWARD_ORDER:
            lag, stage = BACKWARD_LAGS[n], stages[n]
            if 0 <= i - lag < nc:
                stage(i - lag)
    for i, (device, who) in enumerate(score):
        got(SB.at[who], ss.at[i], sr.at[i], device)
    dots = SB[0, :, 0, :] + SB[1, :, 0, :] + SB[2, :, 0, :] + SB[3, :, 0, :]
    fis_ref[0] = jnp.sum((sg[:, 1, :] * dots) ** 2) * (1.0 / 256.0)
    for copy in sent:
        copy.wait_send()


def backward(da, db, sg, un, wg, wu):
    width = wg.shape[0]
    chunks, start = [], 0
    for tiles in BACKWARD_TILES:
        chunks.append((start, tiles * 128))
        start += tiles * 128
    pieces = len(chunks)
    vm = pl.BlockSpec(memory_space=pltpu.VMEM)
    hbm = pl.BlockSpec(memory_space=pl.ANY)
    D = pltpu.SemaphoreType.DMA
    return pl.pallas_call(
        functools.partial(backward_kernel, chunks),
        out_shape=(jax.ShapeDtypeStruct((8, width), BF16), jax.ShapeDtypeStruct((1,), F32)),
        in_specs=[vm, vm, vm, vm, hbm, hbm],
        out_specs=(vm, pl.BlockSpec(memory_space=pltpu.SMEM)),
        scratch_shapes=[
            pltpu.VMEM((NY, 128, width), BF16),
            pltpu.VMEM((2, 128, width // 2), BF16),
            pltpu.VMEM((2, 128, width), BF16),
            pltpu.VMEM((NX, 64, width), BF16), pltpu.VMEM((NX, 64, width), BF16), pltpu.VMEM((NX, 64, width), BF16),
            pltpu.VMEM((3, 64, width), BF16),
            pltpu.VMEM((NZ, 16, width // 2), BF16),
            pltpu.VMEM((7, 16, width // 2), BF16),
            pltpu.VMEM((NY, NY, 8, META), F32),
            pltpu.VMEM((width, 256), BF16), pltpu.VMEM((width, 256), BF16),
            D((pieces, 2)), D((3,)), D((3,)), D((pieces, 4)), D((pieces, 4)), D((pieces,)), D((pieces,)),
            D((pieces, 3)), D((pieces, 3)), D((pieces, 7)), D((pieces, 7)),
        ],
        compiler_params=pltpu.CompilerParams(
            collective_id=2, has_side_effects=True, vmem_limit_bytes=60 << 20
        ),
        name="backward",
    )(da, db, sg, un, wg, wu)


def per_device(tokens, out_grads, expert_ids, gates, w_gate, w_up, w_down):
    group = lax.axis_index("dp")
    ids = lax.dynamic_slice_in_dim(expert_ids, group * 8, 8, 0).astype(BF16)
    own_gates = lax.dynamic_slice_in_dim(gates, group * 8, 8, 0)
    meta = jnp.pad(jnp.concatenate([ids, own_gates], axis=1), ((0, 0), (0, META - 16)))
    blk = jnp.concatenate(
        [jnp.concatenate([meta, meta], axis=0), jnp.concatenate([tokens, out_grads], axis=0)], axis=1
    )
    da, db, sg, un = forward(blk, w_gate[0], w_up[0], w_down[0])
    return backward(da, db, sg, un, w_gate[0], w_up[0])


def solution(mesh):
    placed = (
        P(("expert", "dp"), None), P(("expert", "dp"), None), P("expert", None), P("expert", None),
        P("expert", None, "dp"), P("expert", None, "dp"), P("expert", "dp", None),
    )
    return jax.shard_map(
        per_device, mesh=mesh, in_specs=placed,
        out_specs=(P(("expert", "dp"), None), P("expert")), check_vma=False,
    )
```
